256 devices in a mesh: pts: 32 (over z_lo, y, core), ctr: 8 (over x, z_hi).
Axes of the slice: x: 4, y: 4, z: 8 (z_hi: 2, z_lo: 4; z = z_hi * 4 + z_lo), core: 2. Of those that a mesh axis runs over, the one named last changes fastest.
Arguments:
- points: float32 [90, 65536], P(None, 'pts'), may hold values from -6 to 6
- centre_index: int32 [65536], P(('ctr', 'pts')), may hold values from 0 to 65535, as said below
- inv_scale: float32 [90], replicated, may hold values from 0.08 to 0.3
- left_cols: bfloat16 [64, 65536], P(None, 'pts'), may hold values from -0.375 to 0.375
- right_cols: bfloat16 [64, 65536], P(None, ('ctr', 'pts')), may hold values from -0.375 to 0.375
Outputs:
- point_side: float32 [64, 65536], P(None, 'pts')
- centre_side: float32 [64, 65536], P(None, ('ctr', 'pts'))
The draws below stay inside these ranges and needn't reach their ends.
Inputs may be any that keep to these rules, and one draw needn't show every extreme that they name: `centre_index`: indices of the centres among the 65536 sampled points; repeats may occur, and both 0 and 65535 are taken in every draw.
All inputs are finite; a program needn't handle non-finite values.
Results may differ from the reference program's by a relative error of at most 0.012.
Values may be sent and summed in bfloat16 or wider, within the bound.
A program may use at most 64 MiB of HBM per device.

```python
import math
import jax
import jax.numpy as jnp
from jax import lax

F = 90
R = 64
N = 65536
M = 65536


def draw_centre_index(key, part):
    key = jax.random.fold_in(key, 7)
    first_key, second_key, third_key = jax.random.split(key, 3)
    picks = jax.random.randint(first_key, (M,), 0, N)
    spot_one = jax.random.randint(second_key, (), 0, M)
    spot_two = (spot_one + 1 + jax.random.randint(third_key, (), 0, M - 1)) % M
    places = jnp.arange(M)
    picks = jnp.where(places == spot_one, N - 1, picks)
    picks = jnp.where(places == spot_two, 0, picks)
    return picks.astype(jnp.int32)


def block_scale(stream_key, dims, shards, smallest, largest):
    gain, own = 1.0, jax.random.fold_in(stream_key, 6)
    for position, parts in shards:
        heights = jnp.exp(jax.random.uniform(jax.random.fold_in(own, position), (parts,), jnp.float32, smallest / len(shards), largest / len(shards)))
        gain = gain * jnp.repeat(heights, dims[position] // parts).reshape([-1 if axis == position else 1 for axis in range(len(dims))])
    return gain


def scatter_about(rng, dims, deviation, reach, cuts=(), kind=jnp.bfloat16):
    gain = block_scale(rng, dims, cuts, -0.22, 0.18) if cuts else 1.0
    result = jax.random.normal(rng, dims, jnp.float32) * deviation * gain
    return jnp.minimum(jnp.maximum(result, -reach), reach).astype(kind)


def setup_inputs(seed: int = 0) -> dict:
    splits = jax.random.split(jax.random.key(seed), 6)
    points = scatter_about(splits[0], (F, N), 1.0, 6.0, ((1, 32),), jnp.float32)
    centre_index = draw_centre_index(jax.random.fold_in(splits[5], 71), 0)
    inv_scale = jnp.clip(jnp.exp(jax.random.uniform(splits[2], (F,), jnp.float32, math.log(0.08), math.log(0.3))), 0.08, 0.3)
    left_cols = scatter_about(splits[3], (R, N), (max(N // 256, 16)) ** -0.5, 0.375, ((1, 32),))
    right_cols = scatter_about(splits[4], (R, M), (max(M // 256, 16)) ** -0.5, 0.375, ((1, 256),))
    return dict(points=points, centre_index=centre_index, inv_scale=inv_scale, left_cols=left_cols, right_cols=right_cols)


def tile_of(scaled_blk, norm_blk, scaled_ctr, norm_ctr):
    cross = lax.dot_general(scaled_blk, scaled_ctr, (((0,), (0,)), ((), ())), preferred_element_type=jnp.float32)
    dist = jnp.maximum(norm_blk[:, None] + norm_ctr[None, :] - 2.0 * cross, 0.0)
    return jnp.exp(-0.5 * dist).astype(jnp.bfloat16)


def reference(points, centre_index, inv_scale, left_cols, right_cols):
    centres = jnp.take(points, centre_index, axis=1)
    scale_col = inv_scale[:, None]
    scaled_pts = (points * scale_col).astype(jnp.bfloat16)
    scaled_ctr = (centres * scale_col).astype(jnp.bfloat16)
    norm_pts = jnp.sum(jnp.square(scaled_pts.astype(jnp.float32)), axis=0)
    norm_ctr = jnp.sum(jnp.square(scaled_ctr.astype(jnp.float32)), axis=0)
    block_rows = math.gcd(N, 1024)
    count_blocks = N // block_rows

    def advance(running, number):
        start = (number * block_rows).astype(jnp.int32)
        scaled_blk = lax.dynamic_slice_in_dim(scaled_pts, start, block_rows, 1)
        norm_blk = lax.dynamic_slice_in_dim(norm_pts, start, block_rows, 0)
        left_blk = lax.dynamic_slice_in_dim(left_cols, start, block_rows, 1)
        kernel_tile = tile_of(scaled_blk, norm_blk, scaled_ctr, norm_ctr)
        point_blk = lax.dot_general(right_cols, kernel_tile, (((1,), (1,)), ((), ())), preferred_element_type=jnp.float32)
        running = running + jnp.dot(left_blk, kernel_tile, preferred_element_type=jnp.float32)
        return running, point_blk

    centre_side, point_blocks = lax.scan(advance, jnp.zeros((R, M), jnp.float32), jnp.arange(count_blocks, dtype=jnp.int32))
    point_side = jnp.transpose(point_blocks, (1, 0, 2)).reshape(R, N)
    return point_side, centre_side
```

```python
import functools
import math

import jax
import jax.numpy as jnp
from jax import lax
from jax.experimental import pallas as pl
from jax.experimental.pallas import tpu as pltpu
from jax.sharding import PartitionSpec as P

F32, BF16, I32 = jnp.float32, jnp.bfloat16, jnp.int32
MESH = pl.DeviceIdType.MESH
LOG2E = math.log2(math.e)
FEAT = 90
ROWS = 96
COLS = 64
HERE = 2048
BLK = 256
GROUP = 32
PANELS = 8
SLOTS = 32
VMEM_LIMIT = 56 * 2**20


def pieces(value):
    first = value.astype(BF16).astype(F32)
    second = (value - first).astype(BF16).astype(F32)
    third = (value - first - second).astype(BF16).astype(F32)
    return first, second, third


def barrier_with(peers):
    barrier = pltpu.get_barrier_semaphore()
    total = 0
    for axis, count in peers:
        me = lax.axis_index(axis)

        def greet(step, _, axis=axis, count=count, me=me):
            pl.semaphore_signal(
                barrier, inc=1, device_id={axis: lax.rem(me + step, count)}, device_id_type=MESH
            )
            return 0

        lax.fori_loop(1, count, greet, 0)
        total += count - 1
    pl.semaphore_wait(barrier, total)


def gather_kernel(
    pts_ref, inv_ref, idx_ref, right_ref,
    block_ref, table_ref, flag_ref,
    idx_all, rank_all, cols_s, cols_l, lookup, rows_out, rows_in, flag_mine, flag_all,
    idx_send, idx_recv, row_send, row_recv, flag_send, flag_recv,
):
    me = lax.axis_index("pts")
    panel = lax.axis_index("ctr")
    barrier_with([("pts", GROUP), ("ctr", PANELS)])

    def idx_copy(step):
        return pltpu.make_async_remote_copy(
            src_ref=idx_ref, dst_ref=idx_all.at[me],
            send_sem=idx_send.at[step], recv_sem=idx_recv.at[me],
            device_id={"pts": lax.rem(me + step, GROUP)}, device_id_type=MESH,
        )

    def idx_arrival(step):
        source = lax.rem(me + step, GROUP)
        return pltpu.make_async_remote_copy(
            src_ref=idx_ref, dst_ref=idx_all.at[source],
            send_sem=idx_send.at[step], recv_sem=idx_recv.at[source],
            device_id={"pts": source}, device_id_type=MESH,
        )

    def send_idx(step, _):
        idx_copy(step).start()
        return 0

    lax.fori_loop(1, GROUP, send_idx, 0)
    idx_all[me] = idx_ref[...]

    scaled = (pts_ref[...] * inv_ref[...]).astype(BF16).astype(F32)
    half_norm = jnp.sum(scaled * scaled, axis=0, keepdims=True) * (-0.5 * LOG2E)
    first, second, third = pieces(half_norm)
    ones = jnp.ones((3, HERE), F32)
    cols_s[ROWS:, :] = jnp.zeros((128 - ROWS, HERE), F32)
    cols_l[ROWS:, :] = jnp.zeros((128 - ROWS, HERE), F32)
    cols_s[0:FEAT, :] = scaled
    cols_l[0:FEAT, :] = scaled * LOG2E
    cols_s[FEAT:FEAT + 3, :] = ones
    cols_l[FEAT + 3:ROWS, :] = ones
    for place, piece in enumerate((first, second, third)):
        cols_s[FEAT + 3 + place:FEAT + 4 + place, :] = piece
        cols_l[FEAT + place:FEAT + 1 + place, :] = piece
    for part in range(HERE // 128):
        span = slice(part * 128, (part + 1) * 128)
        high, low = part // 2, (part % 2) * 128
        lookup[low:low + 128, high * 128:(high + 1) * 128] = cols_s[:, span].T.astype(BF16)
        turned = cols_l[:, span].T
        upper = turned.astype(BF16)
        table_ref[span, 0:128] = upper
        table_ref[span, 128:256] = (turned - upper.astype(F32)).astype(BF16)

    before = (
        lax.broadcasted_iota(I32, (BLK, BLK), 0) < lax.broadcasted_iota(I32, (BLK, BLK), 1)
    ).astype(F32).astype(BF16)

    own_idx = idx_ref[...]
    own_owner = own_idx >> 11
    is_owner = lax.broadcasted_iota(I32, (GROUP, BLK), 0) == own_owner
    own_hits = jnp.where(is_owner, 1.0, 0.0)
    own_rank = jnp.dot(own_hits.astype(BF16), before, preferred_element_type=F32)
    own_rank = jnp.sum(own_rank * own_hits, axis=0, keepdims=True).astype(I32)
    own_slot = own_owner * SLOTS + own_rank

    def wait_idx(step, _):
        idx_arrival(step).wait_recv()
        return 0

    lax.fori_loop(1, GROUP, wait_idx, 0)

    idx_rows = jnp.concatenate([idx_all[d] for d in range(GROUP)], axis=0)
    owner = idx_rows >> 11
    hits = jnp.where(owner == me, 1.0, 0.0)
    rank = jnp.dot(hits.astype(BF16), before, preferred_element_type=F32)
    rank = jnp.where(hits > 0.5, rank, -1.0)
    for d in range(GROUP):
        rank_all[d] = rank[d:d + 1, :]

    slot_row = lax.broadcasted_iota(I32, (SLOTS, BLK), 0).astype(F32)
    low_col = lax.broadcasted_iota(I32, (SLOTS, BLK), 1)

    def row_copy(step):
        dest = lax.rem(me + step, GROUP)
        return pltpu.make_async_remote_copy(
            src_ref=rows_out.at[step], dst_ref=rows_in.at[me],
            send_sem=row_send.at[step], recv_sem=row_recv.at[me],
            device_id={"pts": dest}, device_id_type=MESH,
        )

    def row_arrival(step):
        source = lax.rem(me + step, GROUP)
        return pltpu.make_async_remote_copy(
            src_ref=rows_out.at[step], dst_ref=rows_in.at[source],
            send_sem=row_send.at[step], recv_sem=row_recv.at[source],
            device_id={"pts": source}, device_id_type=MESH,
        )

    per = 8

    def look_up(number, _):
        picks, highs = [], []
        for u in range(per):
            dest = lax.rem(me + number * per + u, GROUP)
            local = (idx_all[dest] & (HERE - 1)).astype(F32)
            chosen = rank_all[dest] == slot_row
            key = jnp.sum(jnp.where(chosen, local + 1.0, 0.0), axis=1, keepdims=True)
            key = key.astype(I32) - 1
            highs.append(key >> 8)
            picks.append(jnp.where((key & 255) == low_col, 1.0, 0.0).astype(BF16))
        pick = jnp.concatenate(picks, axis=0)
        high = jnp.concatenate(highs, axis=0)
        found = jnp.dot(pick, lookup[...], preferred_element_type=F32)
        rows = jnp.zeros((per * SLOTS, 128), F32)
        for h in range(8):
            rows = jnp.where(high == h, found[:, h * 128:(h + 1) * 128], rows)
        rows = rows.astype(BF16)
        for u in range(per):
            rows_out[number * per + u] = rows[u * SLOTS:(u + 1) * SLOTS, :]
        for u in range(per):
            step = number * per + u

            @pl.when(step > 0)
            def _():
                row_copy(step).start()

        return 0

    lax.fori_loop(0, GROUP // per, look_up, 0)
    rows_in[me] = rows_out[0]

    def count(source, most):
        here = jnp.sum(jnp.where(owner == source, 1.0, 0.0), axis=1, keepdims=True)
        return jnp.maximum(most, here)

    most = lax.fori_loop(0, GROUP, count, jnp.zeros((GROUP, 1), F32))
    flag_mine[...] = jnp.broadcast_to(jnp.max(most, axis=0, keepdims=True), (8, 128))

    def flag_copy(step):
        return pltpu.make_async_remote_copy(
            src_ref=flag_mine, dst_ref=flag_all.at[panel],
            send_sem=flag_send.at[step], recv_sem=flag_recv.at[panel],
            device_id={"ctr": lax.rem(panel + step, PANELS)}, device_id_type=MESH,
        )

    def flag_arrival(step):
        source = lax.rem(panel + step, PANELS)
        return pltpu.make_async_remote_copy(
            src_ref=flag_mine, dst_ref=flag_all.at[source],
            send_sem=flag_send.at[step], recv_sem=flag_recv.at[source],
            device_id={"ctr": source}, device_id_type=MESH,
        )

    def send_flag(step, _):
        flag_copy(step).start()
        return 0

    lax.fori_loop(1, PANELS, send_flag, 0)
    flag_all[panel] = flag_mine[...]

    place = jnp.where(
        lax.broadcasted_iota(I32, (GROUP * SLOTS, BLK), 0) == own_slot, 1.0, 0.0
    ).astype(BF16)

    def wait_rows(step, _):
        row_arrival(step).wait_recv()
        return 0

    lax.fori_loop(1, GROUP, wait_rows, 0)
    arrived = rows_in[...].reshape(GROUP * SLOTS, 128)
    centres = lax.dot_general(
        arrived, place, (((0,), (0,)), ((), ())), preferred_element_type=F32
    )
    block_ref[0:ROWS, :] = centres[0:ROWS, :].astype(BF16)
    block_ref[ROWS:ROWS + COLS, :] = right_ref[...]

    def wait_flags(step, _):
        flag_arrival(step).wait_recv()
        return 0

    lax.fori_loop(1, PANELS, wait_flags, 0)
    worst = flag_all[0]
    for c in range(1, PANELS):
        worst = jnp.maximum(worst, flag_all[c])
    flag_ref[...] = worst

    def drain(step, _):
        idx_copy(step).wait_send()
        row_copy(step).wait_send()
        return 0

    lax.fori_loop(1, GROUP, drain, 0)

    def drain_flags(step, _):
        flag_copy(step).wait_send()
        return 0

    lax.fori_loop(1, PANELS, drain_flags, 0)


def gather(points, inv_scale, centre_index, right_cols):
    vmem = pl.BlockSpec(memory_space=pltpu.VMEM)
    return pl.pallas_call(
        gather_kernel,
        out_shape=(
            jax.ShapeDtypeStruct((ROWS + COLS, BLK), BF16),
            jax.ShapeDtypeStruct((HERE, 256), BF16),
            jax.ShapeDtypeStruct((8, 128), F32),
        ),
        in_specs=[vmem] * 4,
        out_specs=[vmem] * 3,
        scratch_shapes=[
            pltpu.VMEM((GROUP, 1, BLK), I32),
            pltpu.VMEM((GROUP, 1, BLK), F32),
            pltpu.VMEM((128, HERE), F32),
            pltpu.VMEM((128, HERE), F32),
            pltpu.VMEM((256, 1024), BF16),
            pltpu.VMEM((GROUP, SLOTS, 128), BF16),
            pltpu.VMEM((GROUP, SLOTS, 128), BF16),
            pltpu.VMEM((8, 128), F32),
            pltpu.VMEM((PANELS, 8, 128), F32),
            pltpu.SemaphoreType.DMA((GROUP,)),
            pltpu.SemaphoreType.DMA((GROUP,)),
            pltpu.SemaphoreType.DMA((GROUP,)),
            pltpu.SemaphoreType.DMA((GROUP,)),
            pltpu.SemaphoreType.DMA((PANELS,)),
            pltpu.SemaphoreType.DMA((PANELS,)),
        ],
        compiler_params=pltpu.CompilerParams(
            collective_id=0, has_side_effects=True, vmem_limit_bytes=VMEM_LIMIT
        ),
        name="gather_centres",
    )(points, inv_scale[:, None], centre_index[None, :], right_cols)


def dense_block(points, centre_index, inv_scale, right_cols):
    offset = lax.axis_index("pts") * HERE
    indices = lax.all_gather(centre_index, "pts", axis=0, tiled=True)
    local = indices - offset
    inside = (local >= 0) & (local < HERE)
    taken = jnp.take(points, jnp.clip(local, 0, HERE - 1), axis=1)
    picked = jnp.where(inside[None, :], taken, 0.0)
    raw = lax.psum_scatter(picked, "pts", scatter_dimension=1, tiled=True)
    scaled = lax.reduce_precision(raw * inv_scale[:, None], 8, 7)
    half_norm = jnp.sum(scaled * scaled, axis=0, keepdims=True) * (-0.5 * LOG2E)
    first = lax.reduce_precision(half_norm, 8, 7)
    second = lax.reduce_precision(half_norm - first, 8, 7)
    third = lax.reduce_precision(half_norm - first - second, 8, 7)
    rows = jnp.concatenate([scaled, jnp.ones((3, BLK), F32), first, second, third], axis=0)
    return jnp.concatenate([rows.astype(BF16), right_cols], axis=0)


CHIPS = 16
TILE_I = 1024


def product_kernel(
    block_ref, table_ref, left_ref,
    point_ref, centre_ref,
    blocks, point_acc, mine, for_pair, from_pair, to_home, at_home,
    x_out, x_in, z_out, z_in, back_out, back_in,
    rail_send, pair_send, block_recv, part_send, part_recv, home_send, home_recv,
    x_send, x_recv, z_send, z_recv, back_send, back_recv,
):
    me = lax.axis_index("pts")
    panel = lax.axis_index("ctr")
    z, y, core = me // 8, lax.rem(me // 2, 4), lax.rem(me, 2)
    x, z_hi = panel // 2, lax.rem(panel, 2)

    def at(dz, dy, c):
        return lax.rem(z + dz, 4) * 8 + lax.rem(y + dy, 4) * 2 + c

    def before(dz, dy, c):
        return lax.rem(z + 4 - dz, 4) * 8 + lax.rem(y + 4 - dy, 4) * 2 + c

    other = 1 - core
    pair = {"pts": at(0, 0, other)}
    cross = {"ctr": x * 2 + 1 - z_hi}

    barrier = pltpu.get_barrier_semaphore()

    def greet(m, _):
        pl.semaphore_signal(
            barrier, inc=1, device_id={"pts": at(lax.rem(m, 4), m // 4, core)}, device_id_type=MESH
        )
        return 0

    lax.fori_loop(1, CHIPS, greet, 0)
    pl.semaphore_signal(barrier, inc=1, device_id=pair, device_id_type=MESH)
    pl.semaphore_signal(barrier, inc=1, device_id=cross, device_id_type=MESH)
    for dx in (1, 2, 3):
        pl.semaphore_signal(
            barrier, inc=1, device_id={"ctr": lax.rem(x + dx, 4) * 2 + z_hi}, device_id_type=MESH
        )
    pl.semaphore_wait(barrier, CHIPS - 1 + 5)

    def rail_copy(slot, dz, dy, number):
        return pltpu.make_async_remote_copy(
            src_ref=blocks.at[slot], dst_ref=blocks.at[slot],
            send_sem=rail_send.at[number], recv_sem=block_recv.at[slot],
            device_id={"pts": at(dz, dy, core)}, device_id_type=MESH,
        )

    def pair_copy(slot, m):
        return pltpu.make_async_remote_copy(
            src_ref=blocks.at[slot], dst_ref=blocks.at[slot],
            send_sem=pair_send.at[m], recv_sem=block_recv.at[slot],
            device_id=pair, device_id_type=MESH,
        )

    def pass_on(slot, dz):
        for dy in (1, 2, 3):
            rail_copy(slot, 0, dy, 3 + dz * 3 + dy - 1).start()

    own = at(0, 0, core)
    blocks[own] = block_ref[...]
    pair_copy(own, 0).start()
    for dz in (1, 2, 3):
        rail_copy(own, dz, 0, dz - 1).start()
    pass_on(own, 0)
    point_acc[...] = jnp.zeros_like(point_acc)

    def part_copy(m):
        return pltpu.make_async_remote_copy(
            src_ref=for_pair.at[m], dst_ref=from_pair.at[m],
            send_sem=part_send.at[m], recv_sem=part_recv.at[m],
            device_id=pair, device_id_type=MESH,
        )

    def home_copy(m):
        return pltpu.make_async_remote_copy(
            src_ref=to_home.at[m], dst_ref=at_home.at[m],
            send_sem=home_send.at[m], recv_sem=home_recv.at[m],
            device_id={"pts": at(lax.rem(m, 4), m // 4, core)}, device_id_type=MESH,
        )

    def finish(m):
        part_copy(m).wait_recv()
        to_home[m] = (mine[m] + from_pair[m].astype(F32)).astype(BF16)

    def advance(m, _):
        ahead = m + 1

        @pl.when(ahead < CHIPS)
        def _():
            dz, dy = lax.rem(ahead, 4), ahead // 4
            slot = at(dz, dy, core)
            rail_copy(slot, 0, 0, 0).wait_recv()
            pair_copy(slot, ahead).start()

            @pl.when(ahead < 4)
            def _():
                pass_on(slot, ahead)

        dz, dy = lax.rem(m, 4), m // 4
        slot, pair_slot = at(dz, dy, core), at(dz, dy, other)
        pair_copy(pair_slot, m).wait_recv()

        blank = jnp.zeros((128 - ROWS, BLK), BF16)
        sides, rights = [], []
        for s in (slot, pair_slot):
            cut = blocks[s, 0:ROWS, :]
            sides.append(jnp.concatenate([cut, blank, cut, blank], axis=0))
            rights.append(blocks[s, ROWS:ROWS + COLS, :])
        side = jnp.concatenate(sides, axis=1)
        right = jnp.concatenate(rights, axis=1)
        total = None
        for t in range(HERE // TILE_I):
            span = slice(t * TILE_I, (t + 1) * TILE_I)
            power = jnp.dot(table_ref[span, :], side, preferred_element_type=F32)
            kernel = jnp.exp2(jnp.minimum(power, 0.0)).astype(BF16)
            point_acc[:, span] += lax.dot_general(
                right, kernel, (((1,), (1,)), ((), ())), preferred_element_type=F32
            )
            part = jnp.dot(left_ref[:, span], kernel, preferred_element_type=F32)
            total = part if total is None else total + part
        mine[m] = total[:, 0:BLK]
        for_pair[m] = total[:, BLK:].astype(BF16)
        part_copy(m).start()

        @pl.when(m > 1)
        def _():
            finish(m - 1)
            home_copy(m - 1).start()

        @pl.when(m == 1)
        def _():
            finish(0)

        return 0

    lax.fori_loop(0, CHIPS, advance, 0)

    part = HERE // 4

    def x_copy(dx):
        return pltpu.make_async_remote_copy(
            src_ref=x_out.at[dx - 1], dst_ref=x_in.at[dx - 1],
            send_sem=x_send.at[dx - 1], recv_sem=x_recv.at[dx - 1],
            device_id={"ctr": lax.rem(x + dx, 4) * 2 + z_hi}, device_id_type=MESH,
        )

    def own_part(step):
        return pl.ds(pl.multiple_of(lax.rem(x + step, 4) * part, part), part)

    for dx in (1, 2, 3):
        x_out[dx - 1] = point_acc[:, own_part(dx)].astype(BF16)
        x_copy(dx).start()

    finish(CHIPS - 1)
    home_copy(CHIPS - 1).start()

    total = point_acc[:, own_part(0)]
    for dx in (1, 2, 3):
        x_copy(dx).wait_recv()
        total = total + x_in[dx - 1].astype(F32)
    z_out[...] = total.astype(BF16)
    z_copy = pltpu.make_async_remote_copy(
        src_ref=z_out, dst_ref=z_in, send_sem=z_send, recv_sem=z_recv,
        device_id=cross, device_id_type=MESH,
    )
    z_copy.start()

    def wait_home(m, _):
        home_copy(m).wait_recv()
        return 0

    z_copy.wait_recv()
    back_out[...] = (z_out[...].astype(F32) + z_in[...].astype(F32)).astype(BF16)

    def back_copy(dx):
        return pltpu.make_async_remote_copy(
            src_ref=back_out, dst_ref=back_in.at[dx - 1],
            send_sem=back_send.at[dx - 1], recv_sem=back_recv.at[dx - 1],
            device_id={"ctr": lax.rem(x + dx, 4) * 2 + z_hi}, device_id_type=MESH,
        )

    for dx in (1, 2, 3):
        back_copy(dx).start()
    point_ref[:, own_part(0)] = back_out[...].astype(F32)

    lax.fori_loop(1, CHIPS, wait_home, 0)
    centre = to_home[0].astype(F32)
    for m in range(1, CHIPS):
        centre = centre + at_home[m].astype(F32)
    centre_ref[...] = centre

    for dx in (1, 2, 3):
        back_copy(dx).wait_recv()
        point_ref[:, own_part(4 - dx)] = back_in[dx - 1].astype(F32)

    for number in range(15):
        rail_copy(own, 0, 0, number).wait_send()
    for dx in (1, 2, 3):
        x_copy(dx).wait_send()
        back_copy(dx).wait_send()
    z_copy.wait_send()

    def drain(m, _):
        pair_copy(own, m).wait_send()
        part_copy(m).wait_send()
        return 0

    lax.fori_loop(0, CHIPS, drain, 0)

    def drain_home(m, _):
        home_copy(m).wait_send()
        return 0

    lax.fori_loop(1, CHIPS, drain_home, 0)


def products(block, table, left_cols):
    vmem = pl.BlockSpec(memory_space=pltpu.VMEM)
    dma = pltpu.SemaphoreType.DMA
    part = HERE // 4
    return pl.pallas_call(
        product_kernel,
        out_shape=(
            jax.ShapeDtypeStruct((COLS, HERE), F32),
            jax.ShapeDtypeStruct((COLS, BLK), F32),
        ),
        in_specs=[vmem] * 3,
        out_specs=[vmem] * 2,
        scratch_shapes=[
            pltpu.VMEM((GROUP, ROWS + COLS, BLK), BF16),
            pltpu.VMEM((COLS, HERE), F32),
            pltpu.VMEM((CHIPS, COLS, BLK), F32),
            pltpu.VMEM((CHIPS, COLS, BLK), BF16),
            pltpu.VMEM((CHIPS, COLS, BLK), BF16),
            pltpu.VMEM((CHIPS, COLS, BLK), BF16),
            pltpu.VMEM((CHIPS, COLS, BLK), BF16),
            pltpu.VMEM((3, COLS, part), BF16),
            pltpu.VMEM((3, COLS, part), BF16),
            pltpu.VMEM((COLS, part), BF16),
            pltpu.VMEM((COLS, part), BF16),
            pltpu.VMEM((COLS, part), BF16),
            pltpu.VMEM((3, COLS, part), BF16),
            dma((15,)), dma((CHIPS,)), dma((GROUP,)), dma((CHIPS,)), dma((CHIPS,)),
            dma((CHIPS,)), dma((CHIPS,)),
            dma((3,)), dma((3,)), dma, dma, dma((3,)), dma((3,)),
        ],
        compiler_params=pltpu.CompilerParams(
            collective_id=1, has_side_effects=True, vmem_limit_bytes=VMEM_LIMIT
        ),
        name="kernel_products",
    )(block, table, left_cols)


def body(points, centre_index, inv_scale, left_cols, right_cols):
    block, table, flag = gather(points, inv_scale, centre_index, right_cols)
    block = lax.cond(
        flag[0, 0] > SLOTS,
        lambda: dense_block(points, centre_index, inv_scale, right_cols),
        lambda: block,
    )
    return products(block, table, left_cols)


def solution(mesh):
    return jax.shard_map(
        body,
        mesh=mesh,
        in_specs=(P(None, "pts"), P(("ctr", "pts")), P(), P(None, "pts"), P(None, ("ctr", "pts"))),
        out_specs=(P(None, "pts"), P(None, ("ctr", "pts"))),
        check_vma=False,
    )
```

```python
import math

import jax
import jax.numpy as jnp
from jax import lax
from jax.experimental import pallas as pl
from jax.experimental.pallas import tpu as pltpu
from jax.sharding import PartitionSpec as P

F32, BF16, I32 = jnp.float32, jnp.bfloat16, jnp.int32
MESH = pl.DeviceIdType.MESH
LOG2E = math.log2(math.e)
FEAT = 90
ROWS = 96
COLS = 64
HERE = 2048
BLK = 256
CHIPS = 16
SLOTS = 48
PER = 8
TILE_I = 512
WIDE = 3
PART = HERE // 4
VMEM_LIMIT = 56 * 2**20


def pieces(value):
    first = value.astype(BF16).astype(F32)
    second = (value - first).astype(BF16).astype(F32)
    third = (value - first - second).astype(BF16).astype(F32)
    return first, second, third


def fused_kernel(
    pts_ref, inv_ref, idx_ref, left_ref, right_ref,
    point_ref, centre_ref, flag_ref,
    idx_all, rank_all, cols_s, cols_l, lookup, rows_out, rows_in,
    tables, lefts, blocks, rights, point_acc, own_part, to_home, at_home,
    pair_out, pair_in, x_out, x_in, z_out, z_in, back_out, back_in,
    flag_mine, flag_pair, flag_x, flag_z,
    idx_send, idx_recv, row_send, row_recv, right_send, right_recv,
    block_send, block_recv, home_send, home_recv, pair_send, pair_recv,
    x_send, x_recv, z_send, z_recv, back_send, back_recv, fx_send, fx_recv,
):
    me = lax.axis_index("pts")
    panel = lax.axis_index("ctr")
    chip, core = me // 2, lax.rem(me, 2)
    z, y = chip // 4, lax.rem(chip, 4)
    x, z_hi = panel // 2, lax.rem(panel, 2)
    pair = {"pts": chip * 2 + 1 - core}
    across = {"ctr": x * 2 + 1 - z_hi}

    def chip_at(m):
        return lax.rem(z + lax.rem(m, 4), 4) * 4 + lax.rem(y + m // 4, 4)

    def along_x(dx):
        return {"ctr": lax.rem(x + dx, 4) * 2 + z_hi}

    def remote(src, dst, send, recv, device):
        return pltpu.make_async_remote_copy(
            src_ref=src, dst_ref=dst, send_sem=send, recv_sem=recv,
            device_id=device, device_id_type=MESH,
        )

    def loop(first, last, act):
        def step(m, _):
            act(m)
            return 0

        lax.fori_loop(first, last, step, 0)

    barrier = pltpu.get_barrier_semaphore()
    pl.semaphore_signal(barrier, inc=1, device_id=across, device_id_type=MESH)
    for dx in (1, 2, 3):
        pl.semaphore_signal(barrier, inc=1, device_id=along_x(dx), device_id_type=MESH)
    loop(1, CHIPS, lambda m: pl.semaphore_signal(
        barrier, inc=1, device_id={"pts": chip_at(m) * 2 + core}, device_id_type=MESH
    ))
    pl.semaphore_signal(barrier, inc=1, device_id=pair, device_id_type=MESH)
    pl.semaphore_wait(barrier, CHIPS + 4)

    def rail(src, dst, send, recv, m):
        return remote(src, dst, send.at[m], recv, {"pts": chip_at(m) * 2 + core})

    def idx_copy(m):
        return rail(idx_ref, idx_all.at[chip], idx_send, idx_recv.at[chip], m)

    def idx_arrival(m):
        return rail(idx_ref, idx_all.at[chip_at(m)], idx_send, idx_recv.at[chip_at(m)], m)

    loop(1, CHIPS, lambda m: idx_copy(m).start())
    idx_all[chip] = idx_ref[...]

    eye = lax.broadcasted_iota(I32, (FEAT, FEAT), 0) == lax.broadcasted_iota(I32, (FEAT, FEAT), 1)
    scale = jnp.sum(jnp.where(eye, inv_ref[...], 0.0), axis=1, keepdims=True)
    scaled = (pts_ref[...] * scale).astype(BF16).astype(F32)
    half_norm = jnp.sum(scaled * scaled, axis=0, keepdims=True) * (-0.5 * LOG2E)
    ones = jnp.ones((3, HERE), F32)
    cols_s[ROWS:, :] = jnp.zeros((128 - ROWS, HERE), F32)
    cols_l[ROWS:, :] = jnp.zeros((128 - ROWS, HERE), F32)
    cols_s[0:FEAT, :] = scaled
    cols_l[0:FEAT, :] = scaled * LOG2E
    cols_s[FEAT:FEAT + 3, :] = ones
    cols_l[FEAT + 3:ROWS, :] = ones
    for place, piece in enumerate(pieces(half_norm)):
        cols_s[FEAT + 3 + place:FEAT + 4 + place, :] = piece
        cols_l[FEAT + place:FEAT + 1 + place, :] = piece
    for part in range(HERE // 128):
        span = slice(part * 128, (part + 1) * 128)
        high, low = part // 2, (part % 2) * 128
        lookup[core, low:low + 128, high * 128:(high + 1) * 128] = cols_s[:, span].T.astype(BF16)
    swap_lookup = remote(
        lookup.at[core], lookup.at[core], pair_send.at[0], pair_recv.at[0], pair
    )
    swap_lookup.start()
    for part in range(HERE // 128):
        span = slice(part * 128, (part + 1) * 128)
        turned = cols_l[:, span].T
        upper = turned.astype(BF16)
        tables[0, span, 0:128] = upper
        tables[0, span, 128:256] = (turned - upper.astype(F32)).astype(BF16)
    swap_table = remote(tables.at[0], tables.at[1], pair_send.at[1], pair_recv.at[1], pair)
    swap_table.start()
    swap_left = remote(left_ref, lefts.at[1], pair_send.at[2], pair_recv.at[2], pair)
    swap_left.start()
    lefts[0] = left_ref[...]

    earlier = (
        lax.broadcasted_iota(I32, (BLK, BLK), 0) < lax.broadcasted_iota(I32, (BLK, BLK), 1)
    ).astype(F32).astype(BF16)

    own_owner = idx_ref[...] >> 12
    own_hits = jnp.where(
        lax.broadcasted_iota(I32, (CHIPS, BLK), 0) == own_owner, 1.0, 0.0
    )
    own_rank = jnp.dot(own_hits.astype(BF16), earlier, preferred_element_type=F32)
    own_rank = jnp.sum(own_rank * own_hits, axis=0, keepdims=True).astype(I32)
    own_slot = own_owner * SLOTS + own_rank

    loop(1, CHIPS, lambda m: idx_arrival(m).wait_recv())

    owner = jnp.concatenate([idx_all[d] for d in range(CHIPS)], axis=0) >> 12
    hits = jnp.where(owner == chip, 1.0, 0.0)
    rank = jnp.dot(hits.astype(BF16), earlier, preferred_element_type=F32)
    rank = jnp.where(hits > 0.5, rank, -1.0)
    for d in range(CHIPS):
        rank_all[d] = rank[d:d + 1, :]

    slot_row = lax.broadcasted_iota(I32, (SLOTS, BLK), 0).astype(F32)
    low_col = lax.broadcasted_iota(I32, (SLOTS, BLK), 1)

    def row_copy(m):
        return rail(rows_out.at[m], rows_in.at[chip], row_send, row_recv.at[chip], m)

    def row_arrival(m):
        return rail(
            rows_out.at[m], rows_in.at[chip_at(m)], row_send, row_recv.at[chip_at(m)], m
        )

    swap_lookup.wait_recv()

    def look_up(number):
        picks, highs = [], []
        for u in range(PER):
            home = chip_at(number * PER + u)
            local = (idx_all[home] & (2 * HERE - 1)).astype(F32)
            chosen = rank_all[home] == slot_row
            key = jnp.sum(jnp.where(chosen, local + 1.0, 0.0), axis=1, keepdims=True)
            key = key.astype(I32) - 1
            highs.append(key >> 8)
            picks.append(jnp.where((key & 255) == low_col, 1.0, 0.0).astype(BF16))
        pick = jnp.concatenate(picks, axis=0)
        high = jnp.concatenate(highs, axis=0)
        rows = jnp.zeros((PER * SLOTS, 128), F32)
        for half in range(2):
            found = jnp.dot(pick, lookup[half], preferred_element_type=F32)
            for h in range(8):
                rows = jnp.where(high == half * 8 + h, found[:, h * 128:(h + 1) * 128], rows)
        rows = rows.astype(BF16)
        for u in range(PER):
            rows_out[number * PER + u] = rows[u * SLOTS:(u + 1) * SLOTS, :]
        for u in range(PER):
            m = number * PER + u

            @pl.when(m > 0)
            def _():
                row_copy(m).start()

    loop(0, CHIPS // PER, look_up)
    rows_in[chip] = rows_out[0]

    def right_copy(m):
        return rail(right_ref, rights.at[chip], right_send, right_recv.at[chip], m)

    def right_arrival(m):
        return rail(right_ref, rights.at[chip_at(m)], right_send, right_recv.at[chip_at(m)], m)

    loop(1, CHIPS, lambda m: right_copy(m).start())
    rights[chip] = right_ref[...]

    placed = jnp.where(
        lax.broadcasted_iota(I32, (CHIPS * SLOTS, BLK), 0) == own_slot, 1.0, 0.0
    ).astype(BF16)

    def count(source, most):
        here = jnp.sum(jnp.where(owner == source, 1.0, 0.0), axis=1, keepdims=True)
        return jnp.maximum(most, here)

    most = lax.fori_loop(0, CHIPS, count, jnp.zeros((CHIPS, 1), F32))
    flag_mine[0] = jnp.broadcast_to(jnp.max(most, axis=0, keepdims=True), (8, 128))
    point_acc[...] = jnp.zeros_like(point_acc)

    loop(1, CHIPS, lambda m: row_arrival(m).wait_recv())
    centres = lax.dot_general(
        rows_in[...].reshape(CHIPS * SLOTS, 128), placed,
        (((0,), (0,)), ((), ())), preferred_element_type=F32,
    )
    blocks[chip] = centres[0:ROWS, :].astype(BF16)

    def block_copy(m):
        return rail(blocks.at[chip], blocks.at[chip], block_send, block_recv.at[chip], m)

    def block_arrival(m):
        there = chip_at(m)
        return rail(blocks.at[chip], blocks.at[there], block_send, block_recv.at[there], m)

    loop(1, CHIPS, lambda m: block_copy(m).start())
    swap_table.wait_recv()
    swap_left.wait_recv()

    def home_copy(m):
        return rail(to_home.at[m], at_home.at[m], home_send, home_recv.at[m], m)

    def multiply(numbers):
        blank = jnp.zeros((128 - ROWS, BLK), BF16)
        sides, mates = [], []
        for m in numbers:
            there = chip_at(m)
            cut = blocks[there]
            sides.append(jnp.concatenate([cut, blank, cut, blank], axis=0))
            mates.append(rights[there])
        side = sides[0] if len(sides) == 1 else jnp.concatenate(sides, axis=1)
        mate = mates[0] if len(mates) == 1 else jnp.concatenate(mates, axis=1)
        total = None
        for own in range(2):
            for t in range(HERE // TILE_I):
                span = slice(t * TILE_I, (t + 1) * TILE_I)
                power = jnp.dot(tables[own, span, :], side, preferred_element_type=F32)
                kernel = jnp.exp2(jnp.minimum(power, 0.0)).astype(BF16)
                point_acc[own, :, span] += lax.dot_general(
                    mate, kernel, (((1,), (1,)), ((), ())), preferred_element_type=F32
                )
                part = jnp.dot(lefts[own, :, span], kernel, preferred_element_type=F32)
                total = part if total is None else total + part
        return total

    own_part[...] = multiply([0])

    def advance(number):
        numbers = [number * WIDE + 1 + u for u in range(WIDE)]
        for m in numbers:
            right_arrival(m).wait_recv()
            block_arrival(m).wait_recv()
        total = multiply(numbers)
        for u, m in enumerate(numbers):
            to_home[m] = total[:, u * BLK:(u + 1) * BLK].astype(BF16)
            home_copy(m).start()

    loop(0, (CHIPS - 1) // WIDE, advance)

    pair_out[...] = point_acc[1].astype(BF16)
    swap_points = remote(pair_out, pair_in, pair_send.at[3], pair_recv.at[3], pair)
    swap_points.start()
    swap_flag = remote(flag_mine.at[0], flag_pair, pair_send.at[4], pair_recv.at[4], pair)
    swap_flag.start()

    def x_copy(dx):
        return remote(
            x_out.at[dx - 1], x_in.at[dx - 1], x_send.at[dx - 1], x_recv.at[dx - 1], along_x(dx)
        )

    def flag_x_copy(dx):
        return remote(
            flag_mine.at[1], flag_x.at[dx - 1], fx_send.at[dx - 1], fx_recv.at[dx - 1], along_x(dx)
        )

    def part_of(step):
        return pl.ds(pl.multiple_of(lax.rem(x + step, 4) * PART, PART), PART)

    swap_points.wait_recv()
    for dx in (1, 2, 3):
        span = part_of(dx)
        x_out[dx - 1] = (point_acc[0, :, span] + pair_in[:, span].astype(F32)).astype(BF16)
        x_copy(dx).start()
    swap_flag.wait_recv()
    flag_mine[1] = jnp.maximum(flag_mine[0], flag_pair[...])
    for dx in (1, 2, 3):
        flag_x_copy(dx).start()

    mine = part_of(0)
    total = point_acc[0, :, mine] + pair_in[:, mine].astype(F32)
    worst = flag_mine[1]
    for dx in (1, 2, 3):
        x_copy(dx).wait_recv()
        total = total + x_in[dx - 1].astype(F32)
    z_out[...] = total.astype(BF16)
    swap_z = remote(z_out, z_in, z_send.at[0], z_recv.at[0], across)
    swap_z.start()
    for dx in (1, 2, 3):
        flag_x_copy(dx).wait_recv()
        worst = jnp.maximum(worst, flag_x[dx - 1])
    flag_mine[2] = worst
    flag_across = remote(flag_mine.at[2], flag_z, z_send.at[1], z_recv.at[1], across)
    flag_across.start()

    loop(1, CHIPS, lambda m: home_copy(m).wait_recv())
    centre = own_part[...]
    for m in range(1, CHIPS):
        centre = centre + at_home[m].astype(F32)
    centre_ref[...] = centre

    swap_z.wait_recv()
    back_out[...] = (z_out[...].astype(F32) + z_in[...].astype(F32)).astype(BF16)

    def back_copy(dx):
        return remote(
            back_out, back_in.at[dx - 1], back_send.at[dx - 1], back_recv.at[dx - 1], along_x(dx)
        )

    for dx in (1, 2, 3):
        back_copy(dx).start()
    point_ref[:, mine] = back_out[...].astype(F32)
    flag_across.wait_recv()
    flag_ref[...] = jnp.maximum(flag_mine[2], flag_z[...])

    def drain(m):
        idx_copy(m).wait_send()
        row_copy(m).wait_send()
        right_copy(m).wait_send()
        block_copy(m).wait_send()
        home_copy(m).wait_send()

    loop(1, CHIPS, drain)
    for copy in (swap_lookup, swap_table, swap_left, swap_points, swap_flag, swap_z, flag_across):
        copy.wait_send()
    for dx in (1, 2, 3):
        x_copy(dx).wait_send()
        flag_x_copy(dx).wait_send()

    for dx in (1, 2, 3):
        back_copy(dx).wait_recv()
        point_ref[:, part_of(4 - dx)] = back_in[dx - 1].astype(F32)
    for dx in (1, 2, 3):
        back_copy(dx).wait_send()


def fused(points, centre_index, inv_scale, left_cols, right_cols):
    vmem = pl.BlockSpec(memory_space=pltpu.VMEM)
    dma = pltpu.SemaphoreType.DMA
    buf = pltpu.VMEM
    return pl.pallas_call(
        fused_kernel,
        out_shape=(
            jax.ShapeDtypeStruct((COLS, HERE), F32),
            jax.ShapeDtypeStruct((COLS, BLK), F32),
            jax.ShapeDtypeStruct((8, 128), F32),
        ),
        in_specs=[vmem] * 5,
        out_specs=[vmem] * 3,
        scratch_shapes=[
            buf((CHIPS, 1, BLK), I32),
            buf((CHIPS, 1, BLK), F32),
            buf((128, HERE), F32),
            buf((128, HERE), F32),
            buf((2, 256, 1024), BF16),
            buf((CHIPS, SLOTS, 128), BF16),
            buf((CHIPS, SLOTS, 128), BF16),
            buf((2, HERE, 256), BF16),
            buf((2, COLS, HERE), BF16),
            buf((CHIPS, ROWS, BLK), BF16),
            buf((CHIPS, COLS, BLK), BF16),
            buf((2, COLS, HERE), F32),
            buf((COLS, BLK), F32),
            buf((CHIPS, COLS, BLK), BF16),
            buf((CHIPS, COLS, BLK), BF16),
            buf((COLS, HERE), BF16),
            buf((COLS, HERE), BF16),
            buf((3, COLS, PART), BF16),
            buf((3, COLS, PART), BF16),
            buf((COLS, PART), BF16),
            buf((COLS, PART), BF16),
            buf((COLS, PART), BF16),
            buf((3, COLS, PART), BF16),
            buf((3, 8, 128), F32),
            buf((8, 128), F32),
            buf((3, 8, 128), F32),
            buf((8, 128), F32),
        ]
        + [dma((CHIPS,))] * 10
        + [dma((5,)), dma((5,)), dma((3,)), dma((3,)), dma((2,)), dma((2,))]
        + [dma((3,))] * 4,
        compiler_params=pltpu.CompilerParams(
            collective_id=0, has_side_effects=True, vmem_limit_bytes=VMEM_LIMIT
        ),
        name="nystrom_products",
    )(points, inv_scale[None, :], centre_index[None, :], left_cols, right_cols)


def tile_of(scaled_blk, norm_blk, scaled_ctr, norm_ctr):
    cross = lax.dot_general(
        scaled_blk, scaled_ctr, (((0,), (0,)), ((), ())), preferred_element_type=jnp.float32
    )
    dist = jnp.maximum(norm_blk[:, None] + norm_ctr[None, :] - 2.0 * cross, 0.0)
    return jnp.exp(-0.5 * dist).astype(jnp.bfloat16)


def dense_products(points, centre_index, inv_scale, left_cols, right_cols):
    rows_here = points.shape[1]
    offset = lax.axis_index("pts") * rows_here
    indices = lax.all_gather(centre_index, "pts", axis=0, tiled=True)
    local_idx = indices - offset
    inside = (local_idx >= 0) & (local_idx < rows_here)
    taken_rows = jnp.take(points, jnp.clip(local_idx, 0, rows_here - 1), axis=1)
    picked = jnp.where(inside[None, :], taken_rows, 0.0)
    scale_col = inv_scale[:, None]
    centre_raw = lax.psum(picked, "pts")
    scaled_ctr = (centre_raw * scale_col).astype(jnp.bfloat16)
    panel_cols = lax.all_gather(right_cols, "pts", axis=1, tiled=True)
    norm_ctr = jnp.sum(jnp.square(scaled_ctr.astype(jnp.float32)), axis=0)
    scaled_pts = (points * scale_col).astype(jnp.bfloat16)
    norm_pts = jnp.sum(jnp.square(scaled_pts.astype(jnp.float32)), axis=0)
    width_rows = left_cols.shape[0]
    block_rows = math.gcd(rows_here, 512)
    count_blocks = rows_here // block_rows
    numbers = jnp.arange(count_blocks, dtype=jnp.int32)

    def kernel_at(number):
        start = number * block_rows
        scaled_blk = lax.dynamic_slice_in_dim(scaled_pts, start, block_rows, 1)
        norm_blk = lax.dynamic_slice_in_dim(norm_pts, start, block_rows, 0)
        left_blk = lax.dynamic_slice_in_dim(left_cols, start, block_rows, 1)
        return (tile_of(scaled_blk, norm_blk, scaled_ctr, norm_ctr), left_blk)

    def point_product(kernel_tile):
        return lax.dot_general(
            panel_cols, kernel_tile, (((1,), (1,)), ((), ())), preferred_element_type=jnp.float32
        )

    empty = jnp.zeros((width_rows, scaled_ctr.shape[1]), jnp.float32)

    def advance(running, number):
        kernel_tile, left_blk = kernel_at(number)
        running = running + jnp.dot(left_blk, kernel_tile, preferred_element_type=jnp.float32)
        return (running, point_product(kernel_tile))

    centre_part, point_blocks = lax.scan(advance, empty, numbers)
    point_part = jnp.transpose(point_blocks, (1, 0, 2)).reshape(width_rows, rows_here)
    point_side = lax.psum(point_part, "ctr")
    centre_side = lax.psum_scatter(centre_part, "pts", scatter_dimension=1, tiled=True)
    return (point_side, centre_side)


def body(points, centre_index, inv_scale, left_cols, right_cols):
    point_side, centre_side, flag = fused(points, centre_index, inv_scale, left_cols, right_cols)
    return lax.cond(
        flag[0, 0] > SLOTS,
        lambda: dense_products(points, centre_index, inv_scale, left_cols, right_cols),
        lambda: (point_side, centre_side),
    )


def solution(mesh):
    return jax.shard_map(
        body,
        mesh=mesh,
        in_specs=(P(None, "pts"), P(("ctr", "pts")), P(), P(None, "pts"), P(None, ("ctr", "pts"))),
        out_specs=(P(None, "pts"), P(None, ("ctr", "pts"))),
        check_vma=False,
    )
```

```python
import functools
import math

import jax
import jax.numpy as jnp
from jax import lax
from jax.experimental import pallas as pl
from jax.experimental.pallas import tpu as pltpu
from jax.sharding import PartitionSpec as P

F32, BF16, I32 = jnp.float32, jnp.bfloat16, jnp.int32
MESH = pl.DeviceIdType.MESH
LOG2E = math.log2(math.e)
FEAT = 90
ROWS = 96
COLS = 64
HERE = 2048
BLK = 256
CHIPS = 16
SLOTS = 48
PER = 8
TILE_I = 512
WIDE = 3
PART = HERE // 4
VMEM_LIMIT = 56 * 2**20


def pieces(value):
    first = value.astype(BF16).astype(F32)
    second = (value - first).astype(BF16).astype(F32)
    third = (value - first - second).astype(BF16).astype(F32)
    return first, second, third


def fused_kernel(
    rounds, pts_ref, inv_ref, idx_ref, left_ref, right_ref,
    point_ref, centre_ref, flag_ref,
    idx_all, rank_all, cols_s, cols_l, lookup, rows_out, rows_in,
    tables, lefts, blocks, rights, point_acc, own_part, to_home, at_home,
    pair_out, pair_in, x_out, x_in, z_out, z_in, back_out, back_in,
    flag_mine, flag_pair, flag_x, flag_z,
    idx_send, idx_recv, row_send, row_recv, right_send, right_recv,
    block_send, block_recv, home_send, home_recv, pair_send, pair_recv,
    x_send, x_recv, z_send, z_recv, back_send, back_recv, fx_send, fx_recv,
):
    me = lax.axis_index("pts")
    panel = lax.axis_index("ctr")
    chip, core = me // 2, lax.rem(me, 2)
    z, y = chip // 4, lax.rem(chip, 4)
    x, z_hi = panel // 2, lax.rem(panel, 2)
    pair = {"pts": chip * 2 + 1 - core}
    across = {"ctr": x * 2 + 1 - z_hi}

    def chip_at(m):
        return lax.rem(z + lax.rem(m, 4), 4) * 4 + lax.rem(y + m // 4, 4)

    def along_x(dx):
        return {"ctr": lax.rem(x + dx, 4) * 2 + z_hi}

    def remote(src, dst, send, recv, device):
        return pltpu.make_async_remote_copy(
            src_ref=src, dst_ref=dst, send_sem=send, recv_sem=recv,
            device_id=device, device_id_type=MESH,
        )

    def loop(first, last, act):
        def step(m, _):
            act(m)
            return 0

        lax.fori_loop(first, last, step, 0)

    barrier = pltpu.get_barrier_semaphore()
    pl.semaphore_signal(barrier, inc=1, device_id=across, device_id_type=MESH)
    for dx in (1, 2, 3):
        pl.semaphore_signal(barrier, inc=1, device_id=along_x(dx), device_id_type=MESH)
    loop(1, CHIPS, lambda m: pl.semaphore_signal(
        barrier, inc=1, device_id={"pts": chip_at(m) * 2 + core}, device_id_type=MESH
    ))
    pl.semaphore_signal(barrier, inc=1, device_id=pair, device_id_type=MESH)
    pl.semaphore_wait(barrier, CHIPS + 4)

    def rail(src, dst, send, recv, m):
        return remote(src, dst, send.at[m], recv, {"pts": chip_at(m) * 2 + core})

    def idx_copy(m):
        return rail(idx_ref, idx_all.at[chip], idx_send, idx_recv.at[chip], m)

    def idx_arrival(m):
        return rail(idx_ref, idx_all.at[chip_at(m)], idx_send, idx_recv.at[chip_at(m)], m)

    loop(1, CHIPS, lambda m: idx_copy(m).start())
    idx_all[chip] = idx_ref[...]

    class Spread:
        def __init__(self, held, send, recv):
            self.held, self.send, self.recv = held, send, recv

        def copy(self, m, source):
            there = chip_at(source)
            return rail(self.held.at[there], self.held.at[there], self.send, self.recv.at[there], m)

        def first(self):
            for d in (1, 2, 3):
                self.copy(4 * d, 0).start()
                self.copy(d, 0).start()

        def second(self):
            for dz in (1, 2, 3):
                self.arrive(dz)
                for dy in (1, 2, 3):
                    rail_on = {"pts": chip_at(4 * dy) * 2 + core}
                    there = chip_at(dz)
                    remote(
                        self.held.at[there], self.held.at[there],
                        self.send.at[dz + 4 * dy], self.recv.at[there], rail_on,
                    ).start()

        def arrive(self, m):
            self.copy(m, m).wait_recv()

        def drain(self, m):
            self.copy(m, 0).wait_send()

    right_spread = Spread(rights, right_send, right_recv)
    block_spread = Spread(blocks, block_send, block_recv)
    rights[chip] = right_ref[...]
    right_spread.first()

    eye = lax.broadcasted_iota(I32, (FEAT, FEAT), 0) == lax.broadcasted_iota(I32, (FEAT, FEAT), 1)
    scale = jnp.sum(jnp.where(eye, inv_ref[...], 0.0), axis=1, keepdims=True)
    scaled = (pts_ref[...] * scale).astype(BF16).astype(F32)
    half_norm = jnp.sum(scaled * scaled, axis=0, keepdims=True) * (-0.5 * LOG2E)
    ones = jnp.ones((3, HERE), F32)
    cols_s[ROWS:, :] = jnp.zeros((128 - ROWS, HERE), F32)
    cols_l[ROWS:, :] = jnp.zeros((128 - ROWS, HERE), F32)
    cols_s[0:FEAT, :] = scaled
    cols_l[0:FEAT, :] = scaled * LOG2E
    cols_s[FEAT:FEAT + 3, :] = ones
    cols_l[FEAT + 3:ROWS, :] = ones
    for place, piece in enumerate(pieces(half_norm)):
        cols_s[FEAT + 3 + place:FEAT + 4 + place, :] = piece
        cols_l[FEAT + place:FEAT + 1 + place, :] = piece
    for part in range(HERE // 128):
        span = slice(part * 128, (part + 1) * 128)
        high, low = part // 2, (part % 2) * 128
        lookup[core, low:low + 128, high * 128:(high + 1) * 128] = cols_s[:, span].T.astype(BF16)
    swap_lookup = remote(
        lookup.at[core], lookup.at[core], pair_send.at[0], pair_recv.at[0], pair
    )
    swap_lookup.start()
    for part in range(HERE // 128):
        span = slice(part * 128, (part + 1) * 128)
        turned = cols_l[:, span].T
        upper = turned.astype(BF16)
        tables[0, span, 0:128] = upper
        tables[0, span, 128:256] = (turned - upper.astype(F32)).astype(BF16)
    swap_table = remote(tables.at[0], tables.at[1], pair_send.at[1], pair_recv.at[1], pair)
    swap_table.start()
    swap_left = remote(left_ref, lefts.at[1], pair_send.at[2], pair_recv.at[2], pair)
    swap_left.start()
    lefts[0] = left_ref[...]

    earlier = (
        lax.broadcasted_iota(I32, (BLK, BLK), 0) < lax.broadcasted_iota(I32, (BLK, BLK), 1)
    ).astype(F32).astype(BF16)

    own_owner = idx_ref[...] >> 12
    own_hits = jnp.where(
        lax.broadcasted_iota(I32, (CHIPS, BLK), 0) == own_owner, 1.0, 0.0
    )
    own_rank = jnp.dot(own_hits.astype(BF16), earlier, preferred_element_type=F32)
    own_rank = jnp.sum(own_rank * own_hits, axis=0, keepdims=True).astype(I32)

    loop(1, CHIPS, lambda m: idx_arrival(m).wait_recv())

    owner = jnp.concatenate([idx_all[d] for d in range(CHIPS)], axis=0) >> 12
    hits = jnp.where(owner == chip, 1.0, 0.0)
    rank = jnp.dot(hits.astype(BF16), earlier, preferred_element_type=F32)
    rank = jnp.where(hits > 0.5, rank, -1.0)
    for d in range(CHIPS):
        rank_all[d] = rank[d:d + 1, :]

    slot_row = lax.broadcasted_iota(I32, (SLOTS, BLK), 0).astype(F32)
    low_col = lax.broadcasted_iota(I32, (SLOTS, BLK), 1)

    def row_copy(turn, m):
        return remote(
            rows_out.at[turn, m], rows_in.at[turn, chip],
            row_send.at[turn, m], row_recv.at[turn, chip], {"pts": chip_at(m) * 2 + core},
        )

    def row_arrival(turn, m):
        there = chip_at(m)
        return remote(
            rows_out.at[turn, m], rows_in.at[turn, there],
            row_send.at[turn, m], row_recv.at[turn, there], {"pts": there * 2 + core},
        )

    groups = CHIPS // PER

    def each_round(act):
        for turn in range(rounds):
            loop(1, CHIPS, functools.partial(act, turn))

    swap_lookup.wait_recv()

    def look_up(step):
        turn, number = step // groups, lax.rem(step, groups)
        first_slot = (turn * SLOTS).astype(F32)
        picks, highs = [], []
        for u in range(PER):
            home = chip_at(number * PER + u)
            local = (idx_all[home] & (2 * HERE - 1)).astype(F32)
            chosen = rank_all[home] - first_slot == slot_row
            key = jnp.sum(jnp.where(chosen, local + 1.0, 0.0), axis=1, keepdims=True)
            key = key.astype(I32) - 1
            highs.append(key >> 8)
            picks.append(jnp.where((key & 255) == low_col, 1.0, 0.0).astype(BF16))
        pick = jnp.concatenate(picks, axis=0)
        high = jnp.concatenate(highs, axis=0)
        rows = jnp.zeros((PER * SLOTS, 128), F32)
        for half in range(2):
            found = jnp.dot(pick, lookup[half], preferred_element_type=F32)
            for h in range(8):
                rows = jnp.where(high == half * 8 + h, found[:, h * 128:(h + 1) * 128], rows)
        rows = rows.astype(BF16)
        for u in range(PER):
            rows_out[turn, number * PER + u] = rows[u * SLOTS:(u + 1) * SLOTS, :]
        for u in range(PER):
            m = number * PER + u

            @pl.when(m > 0)
            def _():
                row_copy(turn, m).start()

    loop(0, rounds * groups, look_up)
    for turn in range(rounds):
        rows_in[turn, chip] = rows_out[turn, 0]

    right_spread.second()

    slot = lax.broadcasted_iota(I32, (CHIPS * SLOTS, BLK), 0)
    placed = []
    for turn in range(rounds):
        spot = own_rank - turn * SLOTS
        spot = jnp.where((spot >= 0) & (spot < SLOTS), own_owner * SLOTS + spot, -1)
        placed.append(jnp.where(slot == spot, 1.0, 0.0).astype(BF16))

    def count(source, most):
        here = jnp.sum(jnp.where(owner == source, 1.0, 0.0), axis=1, keepdims=True)
        return jnp.maximum(most, here)

    most = lax.fori_loop(0, CHIPS, count, jnp.zeros((CHIPS, 1), F32))
    flag_mine[0] = jnp.broadcast_to(jnp.max(most, axis=0, keepdims=True), (8, 128))
    point_acc[...] = jnp.zeros_like(point_acc)

    each_round(lambda turn, m: row_arrival(turn, m).wait_recv())
    centres = jnp.zeros((128, BLK), F32)
    for turn in range(rounds):
        centres = centres + lax.dot_general(
            rows_in[turn].reshape(CHIPS * SLOTS, 128), placed[turn],
            (((0,), (0,)), ((), ())), preferred_element_type=F32,
        )
    blocks[chip] = centres[0:ROWS, :].astype(BF16)

    block_spread.first()
    swap_table.wait_recv()
    swap_left.wait_recv()

    def home_copy(m):
        return rail(to_home.at[m], at_home.at[m], home_send, home_recv.at[m], m)

    def multiply(numbers):
        blank = jnp.zeros((128 - ROWS, BLK), BF16)
        sides, mates = [], []
        for m in numbers:
            there = chip_at(m)
            cut = blocks[there]
            sides.append(jnp.concatenate([cut, blank, cut, blank], axis=0))
            mates.append(rights[there])
        side = sides[0] if len(sides) == 1 else jnp.concatenate(sides, axis=1)
        mate = mates[0] if len(mates) == 1 else jnp.concatenate(mates, axis=1)
        total = None
        for own in range(2):
            for t in range(HERE // TILE_I):
                span = slice(t * TILE_I, (t + 1) * TILE_I)
                power = jnp.dot(tables[own, span, :], side, preferred_element_type=F32)
                kernel = jnp.exp2(jnp.minimum(power, 0.0)).astype(BF16)
                point_acc[own, :, span] += lax.dot_general(
                    mate, kernel, (((1,), (1,)), ((), ())), preferred_element_type=F32
                )
                part = jnp.dot(lefts[own, :, span], kernel, preferred_element_type=F32)
                total = part if total is None else total + part
        return total

    own_part[...] = multiply([0])
    block_spread.second()

    def advance(number):
        later = (number + 4) // 5
        numbers = [
            (1 - later) * (u + 1) + later * (number - 1 + 4 * (u + 1)) for u in range(WIDE)
        ]

        @pl.when(number > 0)
        def _():
            for m in numbers:
                right_spread.arrive(m)
                block_spread.arrive(m)

        total = multiply(numbers)
        for u, m in enumerate(numbers):
            to_home[m] = total[:, u * BLK:(u + 1) * BLK].astype(BF16)
            home_copy(m).start()

    loop(0, (CHIPS - 1) // WIDE, advance)

    pair_out[...] = point_acc[1].astype(BF16)
    swap_points = remote(pair_out, pair_in, pair_send.at[3], pair_recv.at[3], pair)
    swap_points.start()
    swap_flag = remote(flag_mine.at[0], flag_pair, pair_send.at[4], pair_recv.at[4], pair)
    swap_flag.start()

    def x_copy(dx):
        return remote(
            x_out.at[dx - 1], x_in.at[dx - 1], x_send.at[dx - 1], x_recv.at[dx - 1], along_x(dx)
        )

    def flag_x_copy(dx):
        return remote(
            flag_mine.at[1], flag_x.at[dx - 1], fx_send.at[dx - 1], fx_recv.at[dx - 1], along_x(dx)
        )

    def part_of(step):
        return pl.ds(pl.multiple_of(lax.rem(x + step, 4) * PART, PART), PART)

    swap_points.wait_recv()
    for dx in (1, 2, 3):
        span = part_of(dx)
        x_out[dx - 1] = (point_acc[0, :, span] + pair_in[:, span].astype(F32)).astype(BF16)
        x_copy(dx).start()
    swap_flag.wait_recv()
    flag_mine[1] = jnp.maximum(flag_mine[0], flag_pair[...])
    for dx in (1, 2, 3):
        flag_x_copy(dx).start()

    mine = part_of(0)
    total = point_acc[0, :, mine] + pair_in[:, mine].astype(F32)
    worst = flag_mine[1]
    for dx in (1, 2, 3):
        x_copy(dx).wait_recv()
        total = total + x_in[dx - 1].astype(F32)
    z_out[...] = total.astype(BF16)
    swap_z = remote(z_out, z_in, z_send.at[0], z_recv.at[0], across)
    swap_z.start()
    for dx in (1, 2, 3):
        flag_x_copy(dx).wait_recv()
        worst = jnp.maximum(worst, flag_x[dx - 1])
    flag_mine[2] = worst
    flag_across = remote(flag_mine.at[2], flag_z, z_send.at[1], z_recv.at[1], across)
    flag_across.start()

    loop(1, CHIPS, lambda m: home_copy(m).wait_recv())
    centre = own_part[...]
    for m in range(1, CHIPS):
        centre = centre + at_home[m].astype(F32)
    centre_ref[...] = centre

    swap_z.wait_recv()
    back_out[...] = (z_out[...].astype(F32) + z_in[...].astype(F32)).astype(BF16)

    def back_copy(dx):
        return remote(
            back_out, back_in.at[dx - 1], back_send.at[dx - 1], back_recv.at[dx - 1], along_x(dx)
        )

    for dx in (1, 2, 3):
        back_copy(dx).start()
    point_ref[:, mine] = back_out[...].astype(F32)
    flag_across.wait_recv()
    flag_ref[...] = jnp.maximum(flag_mine[2], flag_z[...])[0:1, 0:1]

    def drain(m):
        idx_copy(m).wait_send()
        right_spread.drain(m)
        block_spread.drain(m)
        home_copy(m).wait_send()

    loop(1, CHIPS, drain)
    each_round(lambda turn, m: row_copy(turn, m).wait_send())
    for copy in (swap_lookup, swap_table, swap_left, swap_points, swap_flag, swap_z, flag_across):
        copy.wait_send()
    for dx in (1, 2, 3):
        x_copy(dx).wait_send()
        flag_x_copy(dx).wait_send()

    for dx in (1, 2, 3):
        back_copy(dx).wait_recv()
        point_ref[:, part_of(4 - dx)] = back_in[dx - 1].astype(F32)
    for dx in (1, 2, 3):
        back_copy(dx).wait_send()


def fused(rounds, points, centre_index, inv_scale, left_cols, right_cols):
    vmem = pl.BlockSpec(memory_space=pltpu.VMEM)
    dma = pltpu.SemaphoreType.DMA
    buf = pltpu.VMEM
    return pl.pallas_call(
        functools.partial(fused_kernel, rounds),
        out_shape=(
            jax.ShapeDtypeStruct((COLS, HERE), F32),
            jax.ShapeDtypeStruct((COLS, BLK), F32),
            jax.ShapeDtypeStruct((1, 1), F32),
        ),
        in_specs=[vmem] * 5,
        out_specs=[vmem] * 3,
        scratch_shapes=[
            buf((CHIPS, 1, BLK), I32),
            buf((CHIPS, 1, BLK), F32),
            buf((128, HERE), F32),
            buf((128, HERE), F32),
            buf((2, 256, 1024), BF16),
            buf((rounds, CHIPS, SLOTS, 128), BF16),
            buf((rounds, CHIPS, SLOTS, 128), BF16),
            buf((2, HERE, 256), BF16),
            buf((2, COLS, HERE), BF16),
            buf((CHIPS, ROWS, BLK), BF16),
            buf((CHIPS, COLS, BLK), BF16),
            buf((2, COLS, HERE), F32),
            buf((COLS, BLK), F32),
            buf((CHIPS, COLS, BLK), BF16),
            buf((CHIPS, COLS, BLK), BF16),
            buf((COLS, HERE), BF16),
            buf((COLS, HERE), BF16),
            buf((3, COLS, PART), BF16),
            buf((3, COLS, PART), BF16),
            buf((COLS, PART), BF16),
            buf((COLS, PART), BF16),
            buf((COLS, PART), BF16),
            buf((3, COLS, PART), BF16),
            buf((3, 8, 128), F32),
            buf((8, 128), F32),
            buf((3, 8, 128), F32),
            buf((8, 128), F32),
        ]
        + [dma((CHIPS,))] * 2
        + [dma((rounds, CHIPS))] * 2
        + [dma((CHIPS,))] * 6
        + [dma((5,)), dma((5,)), dma((3,)), dma((3,)), dma((2,)), dma((2,))]
        + [dma((3,))] * 4,
        compiler_params=pltpu.CompilerParams(
            collective_id=rounds, has_side_effects=True, vmem_limit_bytes=VMEM_LIMIT
        ),
        name=f"nystrom_products_{rounds}",
    )(points, inv_scale[None, :], centre_index[None, :], left_cols, right_cols)


ROUNDS = -(-BLK // SLOTS)


def body(*arguments):
    point_side, centre_side, most = fused(1, *arguments)
    return lax.cond(
        most[0, 0] > SLOTS, lambda: fused(ROUNDS, *arguments)[:2], lambda: (point_side, centre_side)
    )


def solution(mesh):
    return jax.shard_map(
        body,
        mesh=mesh,
        in_specs=(P(None, "pts"), P(("ctr", "pts")), P(), P(None, "pts"), P(None, ("ctr", "pts"))),
        out_specs=(P(None, "pts"), P(None, ("ctr", "pts"))),
        check_vma=False,
    )
```

```python
import functools
import math

import jax
import jax.numpy as jnp
from jax import lax
from jax.experimental import pallas as pl
from jax.experimental.pallas import tpu as pltpu
from jax.sharding import PartitionSpec as P

F32, BF16, I32 = jnp.float32, jnp.bfloat16, jnp.int32
MESH = pl.DeviceIdType.MESH
LOG2E = math.log2(math.e)
FEAT = 90
ROWS = 96
COLS = 64
HERE = 2048
BLK = 256
CHIPS = 16
SLOTS = 48
PER = 8
PART = HERE // 4
VMEM_LIMIT = 56 * 2**20


def pieces(value):
    first = value.astype(BF16).astype(F32)
    second = (value - first).astype(BF16).astype(F32)
    third = (value - first - second).astype(BF16).astype(F32)
    return first, second, third


def fused_kernel(
    rounds, pts_hbm, inv_hbm, idx_hbm, left_hbm, right_hbm,
    point_hbm, centre_hbm, flag_hbm,
    pts_ref, inv_ref, point_ref, centre_ref, flag_ref, load_sem, store_sem,
    idx_all, rank_all, cols_s, cols_l, lookup, rows_out, rows_in,
    tables, lefts, blocks, rights, point_acc, own_part, to_home, at_home,
    pair_out, pair_in, x_out, x_in, z_out, z_in, back_out, back_in,
    flag_mine, flag_pair, flag_x, flag_z,
    idx_send, idx_recv, row_send, row_recv, right_send, right_recv,
    block_send, block_recv, home_send, home_recv, pair_send, pair_recv,
    x_send, x_recv, z_send, z_recv, back_send, back_recv, fx_send, fx_recv,
):
    me = lax.axis_index("pts")
    panel = lax.axis_index("ctr")
    chip, core = me // 2, lax.rem(me, 2)
    z, y = chip // 4, lax.rem(chip, 4)
    x, z_hi = panel // 2, lax.rem(panel, 2)
    pair = {"pts": chip * 2 + 1 - core}
    across = {"ctr": x * 2 + 1 - z_hi}

    def chip_at(m):
        return lax.rem(z + lax.rem(m, 4), 4) * 4 + lax.rem(y + m // 4, 4)

    def along_x(dx):
        return {"ctr": lax.rem(x + dx, 4) * 2 + z_hi}

    def remote(src, dst, send, recv, device):
        return pltpu.make_async_remote_copy(
            src_ref=src, dst_ref=dst, send_sem=send, recv_sem=recv,
            device_id=device, device_id_type=MESH,
        )

    def loop(first, last, act):
        def step(m, _):
            act(m)
            return 0

        lax.fori_loop(first, last, step, 0)

    loads = [
        pltpu.make_async_copy(source, here, load_sem.at[number])
        for number, (source, here) in enumerate((
            (idx_hbm, idx_all.at[chip]), (right_hbm, rights.at[chip]), (pts_hbm, pts_ref),
            (inv_hbm, inv_ref), (left_hbm, lefts.at[0]),
        ))
    ]
    for load in loads:
        load.start()

    barrier = pltpu.get_barrier_semaphore()
    pl.semaphore_signal(barrier, inc=1, device_id=across, device_id_type=MESH)
    for dx in (1, 2, 3):
        pl.semaphore_signal(barrier, inc=1, device_id=along_x(dx), device_id_type=MESH)
    loop(1, CHIPS, lambda m: pl.semaphore_signal(
        barrier, inc=1, device_id={"pts": chip_at(m) * 2 + core}, device_id_type=MESH
    ))
    pl.semaphore_signal(barrier, inc=1, device_id=pair, device_id_type=MESH)
    pl.semaphore_wait(barrier, CHIPS + 4)

    def rail(src, dst, send, recv, m):
        return remote(src, dst, send.at[m], recv, {"pts": chip_at(m) * 2 + core})

    def idx_copy(m):
        return rail(idx_all.at[chip], idx_all.at[chip], idx_send, idx_recv.at[chip], m)

    def idx_arrival(m):
        there = chip_at(m)
        return rail(idx_all.at[chip], idx_all.at[there], idx_send, idx_recv.at[there], m)

    loads[0].wait()
    loop(1, CHIPS, lambda m: idx_copy(m).start())

    class Spread:
        def __init__(self, held, send, recv):
            self.held, self.send, self.recv = held, send, recv

        def copy(self, m, source):
            there = chip_at(source)
            return rail(self.held.at[there], self.held.at[there], self.send, self.recv.at[there], m)

        def first(self):
            for d in (1, 2, 3):
                self.copy(4 * d, 0).start()
                self.copy(d, 0).start()

        def second(self):
            for dz in (1, 2, 3):
                self.arrive(dz)
                for dy in (1, 2, 3):
                    rail_on = {"pts": chip_at(4 * dy) * 2 + core}
                    there = chip_at(dz)
                    remote(
                        self.held.at[there], self.held.at[there],
                        self.send.at[dz + 4 * dy], self.recv.at[there], rail_on,
                    ).start()

        def arrive(self, m):
            self.copy(m, m).wait_recv()

        def drain(self, m):
            self.copy(m, 0).wait_send()

    right_spread = Spread(rights, right_send, right_recv)
    block_spread = Spread(blocks, block_send, block_recv)
    loads[1].wait()
    right_spread.first()
    loads[2].wait()
    loads[3].wait()

    eye = lax.broadcasted_iota(I32, (FEAT, FEAT), 0) == lax.broadcasted_iota(I32, (FEAT, FEAT), 1)
    scale = jnp.sum(jnp.where(eye, inv_ref[...], 0.0), axis=1, keepdims=True)
    scaled = (pts_ref[...] * scale).astype(BF16).astype(F32)
    half_norm = jnp.sum(scaled * scaled, axis=0, keepdims=True) * (-0.5 * LOG2E)
    ones = jnp.ones((3, HERE), F32)
    cols_s[ROWS:, :] = jnp.zeros((128 - ROWS, HERE), F32)
    cols_l[ROWS:, :] = jnp.zeros((128 - ROWS, HERE), F32)
    cols_s[0:FEAT, :] = scaled
    cols_l[0:FEAT, :] = scaled * LOG2E
    cols_s[FEAT:FEAT + 3, :] = ones
    cols_l[FEAT + 3:ROWS, :] = ones
    for place, piece in enumerate(pieces(half_norm)):
        cols_s[FEAT + 3 + place:FEAT + 4 + place, :] = piece
        cols_l[FEAT + place:FEAT + 1 + place, :] = piece
    for part in range(HERE // 128):
        span = slice(part * 128, (part + 1) * 128)
        high, low = part // 2, (part % 2) * 128
        lookup[core, low:low + 128, high * 128:(high + 1) * 128] = cols_s[:, span].T.astype(BF16)
    swap_lookup = remote(
        lookup.at[core], lookup.at[core], pair_send.at[0], pair_recv.at[0], pair
    )
    swap_lookup.start()
    for part in range(HERE // 128):
        span = slice(part * 128, (part + 1) * 128)
        turned = cols_l[:, span].T
        upper = turned.astype(BF16)
        tables[0, span, 0:128] = upper
        tables[0, span, 128:256] = (turned - upper.astype(F32)).astype(BF16)
    swap_table = remote(tables.at[0], tables.at[1], pair_send.at[1], pair_recv.at[1], pair)
    swap_table.start()
    loads[4].wait()
    swap_left = remote(lefts.at[0], lefts.at[1], pair_send.at[2], pair_recv.at[2], pair)
    swap_left.start()

    earlier = (
        lax.broadcasted_iota(I32, (BLK, BLK), 0) < lax.broadcasted_iota(I32, (BLK, BLK), 1)
    ).astype(F32).astype(BF16)

    own_owner = idx_all[chip] >> 12
    own_hits = jnp.where(
        lax.broadcasted_iota(I32, (CHIPS, BLK), 0) == own_owner, 1.0, 0.0
    )
    own_rank = jnp.dot(own_hits.astype(BF16), earlier, preferred_element_type=F32)
    own_rank = jnp.sum(own_rank * own_hits, axis=0, keepdims=True).astype(I32)

    loop(1, CHIPS, lambda m: idx_arrival(m).wait_recv())

    owner = jnp.concatenate([idx_all[d] for d in range(CHIPS)], axis=0) >> 12
    hits = jnp.where(owner == chip, 1.0, 0.0)
    rank = jnp.dot(hits.astype(BF16), earlier, preferred_element_type=F32)
    rank = jnp.where(hits > 0.5, rank, -1.0)
    for d in range(CHIPS):
        rank_all[d] = rank[d:d + 1, :]

    slot_row = lax.broadcasted_iota(I32, (SLOTS, BLK), 0).astype(F32)
    low_col = lax.broadcasted_iota(I32, (SLOTS, BLK), 1)

    def row_copy(turn, m):
        return remote(
            rows_out.at[turn, m], rows_in.at[turn, chip],
            row_send.at[turn, m], row_recv.at[turn, chip], {"pts": chip_at(m) * 2 + core},
        )

    def row_arrival(turn, m):
        there = chip_at(m)
        return remote(
            rows_out.at[turn, m], rows_in.at[turn, there],
            row_send.at[turn, m], row_recv.at[turn, there], {"pts": there * 2 + core},
        )

    groups = CHIPS // PER

    def each_round(act):
        for turn in range(rounds):
            loop(1, CHIPS, functools.partial(act, turn))

    swap_lookup.wait_recv()

    def look_up(step):
        turn, number = step // groups, lax.rem(step, groups)
        first_slot = (turn * SLOTS).astype(F32)
        picks, highs = [], []
        for u in range(PER):
            home = chip_at(number * PER + u)
            local = (idx_all[home] & (2 * HERE - 1)).astype(F32)
            chosen = rank_all[home] - first_slot == slot_row
            key = jnp.sum(jnp.where(chosen, local + 1.0, 0.0), axis=1, keepdims=True)
            key = key.astype(I32) - 1
            highs.append(key >> 8)
            picks.append(jnp.where((key & 255) == low_col, 1.0, 0.0).astype(BF16))
        pick = jnp.concatenate(picks, axis=0)
        high = jnp.concatenate(highs, axis=0)
        rows = jnp.zeros((PER * SLOTS, 128), F32)
        for half in range(2):
            found = jnp.dot(pick, lookup[half], preferred_element_type=F32)
            for h in range(8):
                rows = jnp.where(high == half * 8 + h, found[:, h * 128:(h + 1) * 128], rows)
        rows = rows.astype(BF16)
        for u in range(PER):
            rows_out[turn, number * PER + u] = rows[u * SLOTS:(u + 1) * SLOTS, :]
        for u in range(PER):
            m = number * PER + u

            @pl.when(m > 0)
            def _():
                row_copy(turn, m).start()

    loop(0, rounds * groups, look_up)
    for turn in range(rounds):
        rows_in[turn, chip] = rows_out[turn, 0]

    right_spread.second()

    slot = lax.broadcasted_iota(I32, (CHIPS * SLOTS, BLK), 0)
    placed = []
    for turn in range(rounds):
        spot = own_rank - turn * SLOTS
        spot = jnp.where((spot >= 0) & (spot < SLOTS), own_owner * SLOTS + spot, -1)
        placed.append(jnp.where(slot == spot, 1.0, 0.0).astype(BF16))

    def count(source, most):
        here = jnp.sum(jnp.where(owner == source, 1.0, 0.0), axis=1, keepdims=True)
        return jnp.maximum(most, here)

    most = lax.fori_loop(0, CHIPS, count, jnp.zeros((CHIPS, 1), F32))
    flag_mine[0] = jnp.broadcast_to(jnp.max(most, axis=0, keepdims=True), (8, 128))
    point_acc[...] = jnp.zeros_like(point_acc)

    each_round(lambda turn, m: row_arrival(turn, m).wait_recv())
    centres = jnp.zeros((128, BLK), F32)
    for turn in range(rounds):
        centres = centres + lax.dot_general(
            rows_in[turn].reshape(CHIPS * SLOTS, 128), placed[turn],
            (((0,), (0,)), ((), ())), preferred_element_type=F32,
        )
    blocks[chip] = centres[0:ROWS, :].astype(BF16)

    block_spread.first()
    swap_table.wait_recv()
    swap_left.wait_recv()

    def home_copy(m):
        return rail(to_home.at[m], at_home.at[m], home_send, home_recv.at[m], m)

    def multiply(numbers, last=None):
        blank = jnp.zeros((128 - ROWS, BLK), BF16)
        sides, mates = [], []
        for m in numbers:
            there = chip_at(m)
            cut = blocks[there]
            sides.append(jnp.concatenate([cut, blank, cut, blank], axis=0))
            mates.append(rights[there])
        side = sides[0] if len(sides) == 1 else jnp.concatenate(sides, axis=1)
        mate = mates[0] if len(mates) == 1 else jnp.concatenate(mates, axis=1)
        def tile(own, span):
            power = jnp.dot(tables[own, span, :], side, preferred_element_type=F32)
            kernel = jnp.exp2(jnp.minimum(power, 0.0)).astype(BF16)
            point_acc[own, :, span] += lax.dot_general(
                mate, kernel, (((1,), (1,)), ((), ())), preferred_element_type=F32
            )
            return jnp.dot(lefts[own, :, span], kernel, preferred_element_type=F32)

        total = None
        for own in (1, 0):
            for t in range(4):
                span = part_of(t + 1) if last and own == 0 else slice(t * PART, (t + 1) * PART)
                part = tile(own, span)
                total = part if total is None else total + part
                if last:
                    last(own, t)
        return total

    def part_of(step):
        return pl.ds(pl.multiple_of(lax.rem(x + step, 4) * PART, PART), PART)

    swap_points = remote(pair_out, pair_in, pair_send.at[3], pair_recv.at[3], pair)
    swap_flag = remote(flag_mine.at[0], flag_pair, pair_send.at[4], pair_recv.at[4], pair)

    def x_copy(dx):
        return remote(
            x_out.at[dx - 1], x_in.at[dx - 1], x_send.at[dx - 1], x_recv.at[dx - 1], along_x(dx)
        )

    def send_x(dx):
        span = part_of(dx)
        x_out[dx - 1] = (point_acc[0, :, span] + pair_in[:, span].astype(F32)).astype(BF16)
        x_copy(dx).start()

    def leave(own, t):
        if (own, t) == (1, 3):
            pair_out[...] = point_acc[1].astype(BF16)
            swap_points.start()
            swap_flag.start()
        if (own, t) == (0, 1):
            swap_points.wait_recv()
            send_x(1)
            send_x(2)
        if (own, t) == (0, 2):
            send_x(3)

    own_part[...] = multiply([0])
    block_spread.second()

    def send_home(total, numbers):
        for u, m in enumerate(numbers):
            to_home[m] = total[:, u * BLK:(u + 1) * BLK].astype(BF16)
            home_copy(m).start()

    def arrive(numbers):
        for m in numbers:
            right_spread.arrive(m)
            block_spread.arrive(m)

    def advance(number):
        later = (number + 3) // 4
        numbers = [
            (1 - later) * (u + 1) + later * (number - 1 + 4 * (u + 1)) for u in range(3)
        ]

        @pl.when(number > 0)
        def _():
            arrive(numbers)

        send_home(multiply(numbers), numbers)

    loop(0, 4, advance)
    numbers = [7, 11, 15]
    arrive(numbers)
    send_home(multiply(numbers, leave), numbers)

    def flag_x_copy(dx):
        return remote(
            flag_mine.at[1], flag_x.at[dx - 1], fx_send.at[dx - 1], fx_recv.at[dx - 1], along_x(dx)
        )

    swap_flag.wait_recv()
    flag_mine[1] = jnp.maximum(flag_mine[0], flag_pair[...])
    for dx in (1, 2, 3):
        flag_x_copy(dx).start()

    mine = part_of(0)
    total = point_acc[0, :, mine] + pair_in[:, mine].astype(F32)
    worst = flag_mine[1]
    for dx in (1, 2, 3):
        x_copy(dx).wait_recv()
        total = total + x_in[dx - 1].astype(F32)
    z_out[...] = total.astype(BF16)
    swap_z = remote(z_out, z_in, z_send.at[0], z_recv.at[0], across)
    swap_z.start()
    for dx in (1, 2, 3):
        flag_x_copy(dx).wait_recv()
        worst = jnp.maximum(worst, flag_x[dx - 1])
    flag_mine[2] = worst
    flag_across = remote(flag_mine.at[2], flag_z, z_send.at[1], z_recv.at[1], across)
    flag_across.start()

    loop(1, CHIPS, lambda m: home_copy(m).wait_recv())
    centre = own_part[...]
    for m in range(1, CHIPS):
        centre = centre + at_home[m].astype(F32)
    centre_ref[...] = centre

    swap_z.wait_recv()
    back_out[...] = (z_out[...].astype(F32) + z_in[...].astype(F32)).astype(BF16)

    def back_copy(dx):
        return remote(
            back_out, back_in.at[dx - 1], back_send.at[dx - 1], back_recv.at[dx - 1], along_x(dx)
        )

    for dx in (1, 2, 3):
        back_copy(dx).start()
    point_ref[:, mine] = back_out[...].astype(F32)
    flag_across.wait_recv()
    flag_ref[...] = jnp.maximum(flag_mine[2], flag_z[...])[0:1, 0:1]
    stores = [
        pltpu.make_async_copy(centre_ref, centre_hbm, store_sem.at[4]),
        pltpu.make_async_copy(flag_ref, flag_hbm, store_sem.at[5]),
    ]
    for store in stores:
        store.start()

    def store_part(step):
        span = part_of(step)
        store = pltpu.make_async_copy(
            point_ref.at[:, span], point_hbm.at[:, span], store_sem.at[step]
        )
        store.start()
        stores.append(store)

    store_part(0)

    def drain(m):
        idx_copy(m).wait_send()
        right_spread.drain(m)
        block_spread.drain(m)
        home_copy(m).wait_send()

    loop(1, CHIPS, drain)
    each_round(lambda turn, m: row_copy(turn, m).wait_send())
    for copy in (swap_lookup, swap_table, swap_left, swap_points, swap_flag, swap_z, flag_across):
        copy.wait_send()
    for dx in (1, 2, 3):
        x_copy(dx).wait_send()
        flag_x_copy(dx).wait_send()

    for dx in (1, 2, 3):
        back_copy(dx).wait_recv()
        point_ref[:, part_of(4 - dx)] = back_in[dx - 1].astype(F32)
        store_part(4 - dx)
    for dx in (1, 2, 3):
        back_copy(dx).wait_send()
    for store in stores:
        store.wait()


def fused(rounds, points, centre_index, inv_scale, left_cols, right_cols):
    anywhere = pl.BlockSpec(memory_space=pl.ANY)
    dma = pltpu.SemaphoreType.DMA
    buf = pltpu.VMEM
    return pl.pallas_call(
        functools.partial(fused_kernel, rounds),
        out_shape=(
            jax.ShapeDtypeStruct((COLS, HERE), F32),
            jax.ShapeDtypeStruct((COLS, BLK), F32),
            jax.ShapeDtypeStruct((1, 1), F32),
        ),
        in_specs=[anywhere] * 5,
        out_specs=[anywhere] * 3,
        scratch_shapes=[
            buf((FEAT, HERE), F32),
            buf((1, FEAT), F32),
            buf((COLS, HERE), F32),
            buf((COLS, BLK), F32),
            buf((1, 1), F32),
            dma((5,)),
            dma((6,)),
            buf((CHIPS, 1, BLK), I32),
            buf((CHIPS, 1, BLK), F32),
            buf((128, HERE), F32),
            buf((128, HERE), F32),
            buf((2, 256, 1024), BF16),
            buf((rounds, CHIPS, SLOTS, 128), BF16),
            buf((rounds, CHIPS, SLOTS, 128), BF16),
            buf((2, HERE, 256), BF16),
            buf((2, COLS, HERE), BF16),
            buf((CHIPS, ROWS, BLK), BF16),
            buf((CHIPS, COLS, BLK), BF16),
            buf((2, COLS, HERE), F32),
            buf((COLS, BLK), F32),
            buf((CHIPS, COLS, BLK), BF16),
            buf((CHIPS, COLS, BLK), BF16),
            buf((COLS, HERE), BF16),
            buf((COLS, HERE), BF16),
            buf((3, COLS, PART), BF16),
            buf((3, COLS, PART), BF16),
            buf((COLS, PART), BF16),
            buf((COLS, PART), BF16),
            buf((COLS, PART), BF16),
            buf((3, COLS, PART), BF16),
            buf((3, 8, 128), F32),
            buf((8, 128), F32),
            buf((3, 8, 128), F32),
            buf((8, 128), F32),
        ]
        + [dma((CHIPS,))] * 2
        + [dma((rounds, CHIPS))] * 2
        + [dma((CHIPS,))] * 6
        + [dma((5,)), dma((5,)), dma((3,)), dma((3,)), dma((2,)), dma((2,))]
        + [dma((3,))] * 4,
        compiler_params=pltpu.CompilerParams(
            collective_id=rounds, has_side_effects=True, vmem_limit_bytes=VMEM_LIMIT
        ),
        name=f"nystrom_products_{rounds}",
    )(points, inv_scale[None, :], centre_index[None, :], left_cols, right_cols)


ROUNDS = -(-BLK // SLOTS)


def body(*arguments):
    point_side, centre_side, most = fused(1, *arguments)
    return lax.cond(
        most[0, 0] > SLOTS, lambda: fused(ROUNDS, *arguments)[:2], lambda: (point_side, centre_side)
    )


def solution(mesh):
    return jax.shard_map(
        body,
        mesh=mesh,
        in_specs=(P(None, "pts"), P(("ctr", "pts")), P(), P(None, "pts"), P(None, ("ctr", "pts"))),
        out_specs=(P(None, "pts"), P(None, ("ctr", "pts"))),
        check_vma=False,
    )
```

```python
import functools
import math

import jax
import jax.numpy as jnp
from jax import lax
from jax.experimental import pallas as pl
from jax.experimental.pallas import tpu as pltpu
from jax.sharding import PartitionSpec as P

F32, BF16, I32 = jnp.float32, jnp.bfloat16, jnp.int32
MESH = pl.DeviceIdType.MESH
LOG2E = math.log2(math.e)
FEAT = 90
ROWS = 96
COLS = 64
HERE = 2048
BLK = 256
CHIPS = 16
SLOTS = 48
PER = 8
PART = HERE // 4
HALF = PART // 2
VMEM_LIMIT = 56 * 2**20


def pieces(value):
    first = value.astype(BF16).astype(F32)
    second = (value - first).astype(BF16).astype(F32)
    third = (value - first - second).astype(BF16).astype(F32)
    return first, second, third


def fused_kernel(
    rounds, pts_hbm, inv_hbm, idx_hbm, left_hbm, right_hbm,
    point_hbm, centre_hbm, flag_hbm,
    pts_ref, inv_ref, centre_ref, flag_ref, load_sem, store_sem,
    idx_all, rank_all, cols_s, lookup, rows_out, rows_in,
    lefts, blocks, rights, point_acc, own_part, to_home, at_home,
    pair_out, pair_in, x_out, x_in, z_out, z_in, back_out,
    flag_mine, flag_pair, flag_x, flag_z,
    idx_send, idx_recv, row_send, row_recv, right_send, right_recv,
    block_send, block_recv, home_send, home_recv, pair_send, pair_recv,
    x_send, x_recv, z_send, z_recv, back_send, back_recv, fx_send, fx_recv,
):
    me = lax.axis_index("pts")
    panel = lax.axis_index("ctr")
    chip, core = me // 2, lax.rem(me, 2)
    z, y = chip // 4, lax.rem(chip, 4)
    x, z_hi = panel // 2, lax.rem(panel, 2)
    pair = {"pts": chip * 2 + 1 - core}
    across = {"ctr": x * 2 + 1 - z_hi}

    def chip_at(m):
        return lax.rem(z + lax.rem(m, 4), 4) * 4 + lax.rem(y + m // 4, 4)

    def along_x(dx):
        return {"ctr": lax.rem(x + dx, 4) * 2 + z_hi}

    def remote(src, dst, send, recv, device):
        return pltpu.make_async_remote_copy(
            src_ref=src, dst_ref=dst, send_sem=send, recv_sem=recv,
            device_id=device, device_id_type=MESH,
        )

    def loop(first, last, act):
        def step(m, _):
            act(m)
            return 0

        lax.fori_loop(first, last, step, 0)

    loads = [
        pltpu.make_async_copy(source, here, load_sem.at[number])
        for number, (source, here) in enumerate((
            (idx_hbm, idx_all.at[chip]), (right_hbm, rights.at[chip]), (pts_hbm, pts_ref),
            (inv_hbm, inv_ref), (left_hbm, lefts.at[0]),
        ))
    ]
    for load in loads:
        load.start()

    barrier = pltpu.get_barrier_semaphore()
    pl.semaphore_signal(barrier, inc=1, device_id=across, device_id_type=MESH)
    for dx in (1, 2, 3):
        pl.semaphore_signal(barrier, inc=1, device_id=along_x(dx), device_id_type=MESH)
    loop(1, CHIPS, lambda m: pl.semaphore_signal(
        barrier, inc=1, device_id={"pts": chip_at(m) * 2 + core}, device_id_type=MESH
    ))
    pl.semaphore_signal(barrier, inc=1, device_id=pair, device_id_type=MESH)
    pl.semaphore_wait(barrier, CHIPS + 4)

    def rail(src, dst, send, recv, m):
        return remote(src, dst, send.at[m], recv, {"pts": chip_at(m) * 2 + core})

    def idx_copy(m):
        return rail(idx_all.at[chip], idx_all.at[chip], idx_send, idx_recv.at[chip], m)

    def idx_arrival(m):
        there = chip_at(m)
        return rail(idx_all.at[chip], idx_all.at[there], idx_send, idx_recv.at[there], m)

    loads[0].wait()
    loop(1, CHIPS, lambda m: idx_copy(m).start())

    class Spread:
        def __init__(self, held, send, recv):
            self.held, self.send, self.recv = held, send, recv

        def copy(self, m, source):
            there = chip_at(source)
            return rail(self.held.at[there], self.held.at[there], self.send, self.recv.at[there], m)

        def first(self):
            for d in (1, 2, 3):
                self.copy(d, 0).start()
            for d in (1, 2, 3):
                self.copy(4 * d, 0).start()

        def second(self):
            for dz in (1, 2, 3):
                self.arrive(dz)
                for dy in (1, 2, 3):
                    rail_on = {"pts": chip_at(4 * dy) * 2 + core}
                    there = chip_at(dz)
                    remote(
                        self.held.at[there], self.held.at[there],
                        self.send.at[dz + 4 * dy], self.recv.at[there], rail_on,
                    ).start()

        def arrive(self, m):
            self.copy(m, m).wait_recv()

        def drain(self, m):
            self.copy(m, 0).wait_send()

    right_spread = Spread(rights, right_send, right_recv)
    block_spread = Spread(blocks, block_send, block_recv)
    loads[1].wait()
    right_spread.first()
    loads[2].wait()
    loads[3].wait()

    eye = lax.broadcasted_iota(I32, (FEAT, FEAT), 0) == lax.broadcasted_iota(I32, (FEAT, FEAT), 1)
    scale = jnp.sum(jnp.where(eye, inv_ref[...], 0.0), axis=1, keepdims=True)
    scaled = (pts_ref[...] * scale).astype(BF16).astype(F32)
    half_norm = jnp.sum(scaled * scaled, axis=0, keepdims=True) * -0.5
    cols_s[ROWS:, :] = jnp.zeros((128 - ROWS, HERE), F32)
    cols_s[0:FEAT, :] = scaled
    cols_s[FEAT:FEAT + 3, :] = jnp.ones((3, HERE), F32)
    for place, piece in enumerate(pieces(half_norm)):
        cols_s[FEAT + 3 + place:FEAT + 4 + place, :] = piece
    for part in range(HERE // 128):
        span = slice(part * 128, (part + 1) * 128)
        high, low = part // 2, (part % 2) * 128
        lookup[core, high, low:low + 128, :] = cols_s[:, span].T.astype(BF16)
    swap_lookup = remote(
        lookup.at[core], lookup.at[core], pair_send.at[0], pair_recv.at[0], pair
    )
    swap_lookup.start()
    loads[4].wait()
    swap_left = remote(lefts.at[0], lefts.at[1], pair_send.at[2], pair_recv.at[2], pair)
    swap_left.start()

    earlier = (
        lax.broadcasted_iota(I32, (BLK, BLK), 0) < lax.broadcasted_iota(I32, (BLK, BLK), 1)
    ).astype(F32).astype(BF16)

    own_owner = idx_all[chip] >> 12
    own_hits = jnp.where(
        lax.broadcasted_iota(I32, (CHIPS, BLK), 0) == own_owner, 1.0, 0.0
    )
    own_rank = jnp.dot(own_hits.astype(BF16), earlier, preferred_element_type=F32)
    own_rank = jnp.sum(own_rank * own_hits, axis=0, keepdims=True).astype(I32)

    loop(1, CHIPS, lambda m: idx_arrival(m).wait_recv())

    owner = jnp.concatenate([idx_all[d] for d in range(CHIPS)], axis=0) >> 12
    hits = jnp.where(owner == chip, 1.0, 0.0)
    rank = jnp.dot(hits.astype(BF16), earlier, preferred_element_type=F32)
    rank = jnp.where(hits > 0.5, rank, -1.0)
    for d in range(CHIPS):
        rank_all[d] = rank[d:d + 1, :]

    slot_row = lax.broadcasted_iota(I32, (SLOTS, BLK), 0).astype(F32)
    low_col = lax.broadcasted_iota(I32, (SLOTS, BLK), 1)

    def row_copy(turn, m):
        return remote(
            rows_out.at[turn, m], rows_in.at[turn, chip],
            row_send.at[turn, m], row_recv.at[turn, chip], {"pts": chip_at(m) * 2 + core},
        )

    def row_arrival(turn, m):
        there = chip_at(m)
        return remote(
            rows_out.at[turn, m], rows_in.at[turn, there],
            row_send.at[turn, m], row_recv.at[turn, there], {"pts": there * 2 + core},
        )

    groups = CHIPS // PER

    def each_round(act):
        for turn in range(rounds):
            loop(1, CHIPS, functools.partial(act, turn))

    swap_lookup.wait_recv()

    def look_up(step):
        turn, number = step // groups, lax.rem(step, groups)
        first_slot = (turn * SLOTS).astype(F32)
        picks, highs = [], []
        for u in range(PER):
            home = chip_at(number * PER + u)
            local = (idx_all[home] & (2 * HERE - 1)).astype(F32)
            chosen = rank_all[home] - first_slot == slot_row
            key = jnp.sum(jnp.where(chosen, local + 1.0, 0.0), axis=1, keepdims=True)
            key = key.astype(I32) - 1
            highs.append(key >> 8)
            picks.append(jnp.where((key & 255) == low_col, 1.0, 0.0).astype(BF16))
        pick = jnp.concatenate(picks, axis=0)
        high = jnp.concatenate(highs, axis=0)
        rows = jnp.zeros((PER * SLOTS, 128), F32)
        for half in range(2):
            table = jnp.concatenate([lookup[half, h] for h in range(8)], axis=1)
            found = jnp.dot(pick, table, preferred_element_type=F32)
            for h in range(8):
                rows = jnp.where(high == half * 8 + h, found[:, h * 128:(h + 1) * 128], rows)
        rows = rows.astype(BF16)
        for u in range(PER):
            rows_out[turn, number * PER + u] = rows[u * SLOTS:(u + 1) * SLOTS, :]
        for u in range(PER):
            m = number * PER + u

            @pl.when(m > 0)
            def _():
                row_copy(turn, m).start()

    loop(0, rounds * groups, look_up)
    for turn in range(rounds):
        rows_in[turn, chip] = rows_out[turn, 0]

    right_spread.second()

    slot = lax.broadcasted_iota(I32, (CHIPS * SLOTS, BLK), 0)
    placed = []
    for turn in range(rounds):
        spot = own_rank - turn * SLOTS
        spot = jnp.where((spot >= 0) & (spot < SLOTS), own_owner * SLOTS + spot, -1)
        placed.append(jnp.where(slot == spot, 1.0, 0.0).astype(BF16))

    def count(source, most):
        here = jnp.sum(jnp.where(owner == source, 1.0, 0.0), axis=1, keepdims=True)
        return jnp.maximum(most, here)

    most = lax.fori_loop(0, CHIPS, count, jnp.zeros((CHIPS, 1), F32))
    flag_mine[0] = jnp.broadcast_to(jnp.max(most, axis=0, keepdims=True), (8, 128))
    point_acc[...] = jnp.zeros_like(point_acc)

    each_round(lambda turn, m: row_arrival(turn, m).wait_recv())
    centres = jnp.zeros((128, BLK), F32)
    for turn in range(rounds):
        centres = centres + lax.dot_general(
            rows_in[turn].reshape(CHIPS * SLOTS, 128), placed[turn],
            (((0,), (0,)), ((), ())), preferred_element_type=F32,
        )
    here = slice(0, BLK)
    cols_s[0:ROWS, here] = centres[0:ROWS, :]
    norm_rows = cols_s[FEAT + 3:ROWS, here]
    cols_s[FEAT + 3:ROWS, here] = cols_s[FEAT:FEAT + 3, here]
    cols_s[FEAT:FEAT + 3, here] = norm_rows
    blocks[chip] = cols_s[0:ROWS, here].astype(BF16)

    block_spread.first()
    swap_left.wait_recv()

    def home_copy(m):
        return rail(to_home.at[m], at_home.at[m], home_send, home_recv.at[m], m)

    def multiply(numbers, last=None):
        blank = jnp.zeros((128 - ROWS, BLK), BF16)
        sides, mates = [], []
        for m in numbers:
            there = chip_at(m)
            cut = blocks[there]
            sides.append(jnp.concatenate([cut, blank], axis=0))
            mates.append(rights[there])
        side = sides[0] if len(sides) == 1 else jnp.concatenate(sides, axis=1)
        mate = mates[0] if len(mates) == 1 else jnp.concatenate(mates, axis=1)
        def tile(own, q, span):
            holder = core if own == 0 else 1 - core
            rows = jnp.concatenate([lookup[holder, 2 * q], lookup[holder, 2 * q + 1]], axis=0)
            power = jnp.dot(rows, side, preferred_element_type=F32) * LOG2E
            kernel = jnp.exp2(jnp.minimum(power, 0.0)).astype(BF16)
            point_acc[own, :, span] += lax.dot_general(
                mate, kernel, (((1,), (1,)), ((), ())), preferred_element_type=F32
            )
            return jnp.dot(lefts[own, :, span], kernel, preferred_element_type=F32)

        total = None
        for own in (1, 0):
            for t in range(4):
                if last and own == 0:
                    part = tile(own, lax.rem(x + t + 1, 4), part_of(t + 1))
                else:
                    part = tile(own, t, slice(t * PART, (t + 1) * PART))
                total = part if total is None else total + part
                if last:
                    last(own, t)
        return total

    def part_of(step):
        return pl.ds(pl.multiple_of(lax.rem(x + step, 4) * PART, PART), PART)

    swap_points = remote(pair_out, pair_in, pair_send.at[3], pair_recv.at[3], pair)
    swap_flag = remote(flag_mine.at[0], flag_pair, pair_send.at[4], pair_recv.at[4], pair)

    def half_of(step, half):
        start = lax.rem(x + step, 4) * PART + half * HALF
        return pl.ds(pl.multiple_of(start, HALF), HALF)

    def x_copy(dx, half):
        return remote(
            x_out.at[dx - 1, half], x_in.at[dx - 1, half],
            x_send.at[dx - 1, half], x_recv.at[dx - 1, half], along_x(dx),
        )

    def chip_sum(dx, half):
        span = half_of(dx, half)
        return point_acc[0, :, span] + pair_in[:, span].astype(F32)

    def send_x(dx):
        for half in range(2):
            x_out[dx - 1, half] = chip_sum(dx, half).astype(BF16)
            x_copy(dx, half).start()

    def leave(own, t):
        if (own, t) == (1, 3):
            pair_out[...] = point_acc[1].astype(BF16)
            swap_points.start()
            swap_flag.start()
        if (own, t) == (0, 1):
            swap_points.wait_recv()
            send_x(1)
            send_x(2)
        if (own, t) == (0, 2):
            send_x(3)

    own_part[...] = multiply([0])
    block_spread.second()

    def send_home(total, numbers):
        for u, m in enumerate(numbers):
            to_home[m] = total[:, u * BLK:(u + 1) * BLK].astype(BF16)
            home_copy(m).start()

    def arrive(numbers):
        for m in numbers:
            right_spread.arrive(m)
            block_spread.arrive(m)

    def advance(number):
        later = (number + 3) // 4
        numbers = [
            (1 - later) * (u + 1) + later * (number + 4 * (u + 1)) for u in range(3)
        ]

        @pl.when(number > 0)
        def _():
            arrive(numbers)

        send_home(multiply(numbers), numbers)

    loop(0, 4, advance)
    numbers = [4, 8, 12]
    arrive(numbers)
    send_home(multiply(numbers, leave), numbers)

    def flag_x_copy(dx):
        return remote(
            flag_mine.at[1], flag_x.at[dx - 1], fx_send.at[dx - 1], fx_recv.at[dx - 1], along_x(dx)
        )

    swap_flag.wait_recv()
    flag_mine[1] = jnp.maximum(flag_mine[0], flag_pair[...])
    for dx in (1, 2, 3):
        flag_x_copy(dx).start()

    worst = flag_mine[1]
    swap_z = [
        remote(z_out.at[half], z_in.at[half], z_send.at[half], z_recv.at[half], across)
        for half in range(2)
    ]
    for half in range(2):
        total = chip_sum(0, half)
        for dx in (1, 2, 3):
            x_copy(dx, half).wait_recv()
            total = total + x_in[dx - 1, half].astype(F32)
        z_out[half] = total.astype(BF16)
        swap_z[half].start()
    for dx in (1, 2, 3):
        flag_x_copy(dx).wait_recv()
        worst = jnp.maximum(worst, flag_x[dx - 1])
    flag_mine[2] = worst
    flag_across = remote(flag_mine.at[2], flag_z, z_send.at[2], z_recv.at[2], across)
    flag_across.start()

    loop(1, CHIPS, lambda m: home_copy(m).wait_recv())
    centre = own_part[...]
    for m in range(1, CHIPS):
        centre = centre + at_home[m].astype(F32)
    centre_ref[...] = centre

    def back_copy(dx, half):
        return remote(
            back_out.at[half], point_hbm.at[:, half_of(0, half)],
            back_send.at[dx - 1, half], back_recv.at[dx - 1, half], along_x(dx),
        )

    stores = []
    for half in range(2):
        swap_z[half].wait_recv()
        back_out[half] = (z_out[half].astype(F32) + z_in[half].astype(F32)).astype(BF16)
        for dx in (1, 2, 3):
            back_copy(dx, half).start()
        stores.append(pltpu.make_async_copy(
            back_out.at[half], point_hbm.at[:, half_of(0, half)], store_sem.at[half]
        ))
    flag_across.wait_recv()
    flag_ref[...] = jnp.maximum(flag_mine[2], flag_z[...])[0:1, 0:1]
    stores += [
        pltpu.make_async_copy(centre_ref, centre_hbm, store_sem.at[4]),
        pltpu.make_async_copy(flag_ref, flag_hbm, store_sem.at[5]),
    ]
    for store in stores:
        store.start()

    def drain(m):
        idx_copy(m).wait_send()
        right_spread.drain(m)
        block_spread.drain(m)
        home_copy(m).wait_send()

    loop(1, CHIPS, drain)
    each_round(lambda turn, m: row_copy(turn, m).wait_send())
    for copy in (swap_lookup, swap_left, swap_points, swap_flag, *swap_z, flag_across):
        copy.wait_send()
    for dx in (1, 2, 3):
        for half in range(2):
            x_copy(dx, half).wait_send()
        flag_x_copy(dx).wait_send()

    for half in range(2):
        for dx in (1, 2, 3):
            remote(
                back_out.at[half], point_hbm.at[:, half_of(4 - dx, half)],
                back_send.at[dx - 1, half], back_recv.at[dx - 1, half], along_x(dx),
            ).wait_recv()
            back_copy(dx, half).wait_send()
    for store in stores:
        store.wait()


def fused(rounds, points, centre_index, inv_scale, left_cols, right_cols):
    anywhere = pl.BlockSpec(memory_space=pl.ANY)
    dma = pltpu.SemaphoreType.DMA
    buf = pltpu.VMEM
    return pl.pallas_call(
        functools.partial(fused_kernel, rounds),
        out_shape=(
            jax.ShapeDtypeStruct((COLS, HERE), BF16),
            jax.ShapeDtypeStruct((COLS, BLK), F32),
            jax.ShapeDtypeStruct((1, 1), F32),
        ),
        in_specs=[anywhere] * 5,
        out_specs=[anywhere] * 3,
        scratch_shapes=[
            buf((FEAT, HERE), F32),
            buf((1, FEAT), F32),
            buf((COLS, BLK), F32),
            buf((1, 1), F32),
            dma((5,)),
            dma((6,)),
            buf((CHIPS, 1, BLK), I32),
            buf((CHIPS, 1, BLK), F32),
            buf((128, HERE), F32),
            buf((2, 8, 256, 128), BF16),
            buf((rounds, CHIPS, SLOTS, 128), BF16),
            buf((rounds, CHIPS, SLOTS, 128), BF16),
            buf((2, COLS, HERE), BF16),
            buf((CHIPS, ROWS, BLK), BF16),
            buf((CHIPS, COLS, BLK), BF16),
            buf((2, COLS, HERE), F32),
            buf((COLS, BLK), F32),
            buf((CHIPS, COLS, BLK), BF16),
            buf((CHIPS, COLS, BLK), BF16),
            buf((COLS, HERE), BF16),
            buf((COLS, HERE), BF16),
            buf((3, 2, COLS, HALF), BF16),
            buf((3, 2, COLS, HALF), BF16),
            buf((2, COLS, HALF), BF16),
            buf((2, COLS, HALF), BF16),
            buf((2, COLS, HALF), BF16),
            buf((3, 8, 128), F32),
            buf((8, 128), F32),
            buf((3, 8, 128), F32),
            buf((8, 128), F32),
        ]
        + [dma((CHIPS,))] * 2
        + [dma((rounds, CHIPS))] * 2
        + [dma((CHIPS,))] * 6
        + [dma((5,)), dma((5,)), dma((3, 2)), dma((3, 2)), dma((3,)), dma((3,))]
        + [dma((3, 2))] * 2
        + [dma((3,))] * 2,
        compiler_params=pltpu.CompilerParams(
            collective_id=rounds, has_side_effects=True, vmem_limit_bytes=VMEM_LIMIT
        ),
        name=f"nystrom_products_{rounds}",
    )(points, inv_scale[None, :], centre_index[None, :], left_cols, right_cols)


ROUNDS = -(-BLK // SLOTS)


def body(*arguments):
    point_side, centre_side, most = fused(1, *arguments)
    point_side, centre_side = lax.cond(
        most[0, 0] > SLOTS, lambda: fused(ROUNDS, *arguments)[:2], lambda: (point_side, centre_side)
    )
    return point_side.astype(F32), centre_side


def solution(mesh):
    return jax.shard_map(
        body,
        mesh=mesh,
        in_specs=(P(None, "pts"), P(("ctr", "pts")), P(), P(None, "pts"), P(None, ("ctr", "pts"))),
        out_specs=(P(None, "pts"), P(None, ("ctr", "pts"))),
        check_vma=False,
    )
```

```python
import functools
import math

import jax
import jax.numpy as jnp
from jax import lax
from jax.experimental import pallas as pl
from jax.experimental.pallas import tpu as pltpu
from jax.sharding import PartitionSpec as P

F32, BF16, I32 = jnp.float32, jnp.bfloat16, jnp.int32
MESH = pl.DeviceIdType.MESH
LOG2E = math.log2(math.e)
FEAT = 90
ROWS = 96
COLS = 64
HERE = 2048
BLK = 256
CHIPS = 16
SLOTS = 48
PER = 8
PART = HERE // 4
HALF = PART // 2
VMEM_LIMIT = 56 * 2**20


def pieces(value):
    first = value.astype(BF16).astype(F32)
    second = (value - first).astype(BF16).astype(F32)
    third = (value - first - second).astype(BF16).astype(F32)
    return first, second, third


def fused_kernel(
    rounds, pts_hbm, inv_hbm, idx_hbm, left_hbm, right_hbm,
    point_hbm, centre_hbm, flag_hbm,
    pts_ref, inv_ref, centre_ref, flag_ref, load_sem, store_sem,
    idx_all, rank_all, cols_s, lookup, rows_out, rows_in,
    lefts, blocks, rights, point_acc, own_part, to_home, at_home,
    pair_out, pair_in, x_out, x_in, z_out, z_in, back_out,
    flag_mine, flag_pair, flag_x, flag_z,
    idx_send, idx_recv, row_send, row_recv, right_send, right_recv,
    block_send, block_recv, home_send, home_recv, pair_send, pair_recv,
    part_send, part_recv, x_send, x_recv, z_send, z_recv, back_send, back_recv, fx_send, fx_recv,
):
    me = lax.axis_index("pts")
    panel = lax.axis_index("ctr")
    chip, core = me // 2, lax.rem(me, 2)
    z, y = chip // 4, lax.rem(chip, 4)
    x, z_hi = panel // 2, lax.rem(panel, 2)
    pair = {"pts": chip * 2 + 1 - core}
    across = {"ctr": x * 2 + 1 - z_hi}

    def chip_at(m):
        return lax.rem(z + lax.rem(m, 4), 4) * 4 + lax.rem(y + m // 4, 4)

    def along_x(dx):
        return {"ctr": lax.rem(x + dx, 4) * 2 + z_hi}

    def remote(src, dst, send, recv, device):
        return pltpu.make_async_remote_copy(
            src_ref=src, dst_ref=dst, send_sem=send, recv_sem=recv,
            device_id=device, device_id_type=MESH,
        )

    def loop(first, last, act):
        def step(m, _):
            act(m)
            return 0

        lax.fori_loop(first, last, step, 0)

    loads = [
        pltpu.make_async_copy(source, here, load_sem.at[number])
        for number, (source, here) in enumerate((
            (idx_hbm, idx_all.at[chip]), (right_hbm, rights.at[chip]), (pts_hbm, pts_ref),
            (inv_hbm, inv_ref), (left_hbm, lefts.at[0]),
        ))
    ]
    for load in loads:
        load.start()

    barrier = pltpu.get_barrier_semaphore()
    pl.semaphore_signal(barrier, inc=1, device_id=across, device_id_type=MESH)
    for dx in (1, 2, 3):
        pl.semaphore_signal(barrier, inc=1, device_id=along_x(dx), device_id_type=MESH)
    loop(1, CHIPS, lambda m: pl.semaphore_signal(
        barrier, inc=1, device_id={"pts": chip_at(m) * 2 + core}, device_id_type=MESH
    ))
    pl.semaphore_signal(barrier, inc=1, device_id=pair, device_id_type=MESH)
    pl.semaphore_wait(barrier, CHIPS + 4)

    def rail(src, dst, send, recv, m):
        return remote(src, dst, send.at[m], recv, {"pts": chip_at(m) * 2 + core})

    def idx_copy(m):
        return rail(idx_all.at[chip], idx_all.at[chip], idx_send, idx_recv.at[chip], m)

    def idx_arrival(m):
        there = chip_at(m)
        return rail(idx_all.at[chip], idx_all.at[there], idx_send, idx_recv.at[there], m)

    loads[0].wait()
    loop(1, CHIPS, lambda m: idx_copy(m).start())

    class Spread:
        def __init__(self, held, send, recv):
            self.held, self.send, self.recv = held, send, recv

        def copy(self, m, source):
            there = chip_at(source)
            return rail(self.held.at[there], self.held.at[there], self.send, self.recv.at[there], m)

        def first(self):
            for d in (1, 2, 3):
                self.copy(d, 0).start()
            for d in (1, 2, 3):
                self.copy(4 * d, 0).start()

        def second(self):
            for dz in (1, 2, 3):
                self.arrive(dz)
                for dy in (1, 2, 3):
                    rail_on = {"pts": chip_at(4 * dy) * 2 + core}
                    there = chip_at(dz)
                    remote(
                        self.held.at[there], self.held.at[there],
                        self.send.at[dz + 4 * dy], self.recv.at[there], rail_on,
                    ).start()

        def arrive(self, m):
            self.copy(m, m).wait_recv()

        def drain(self, m):
            self.copy(m, 0).wait_send()

    right_spread = Spread(rights, right_send, right_recv)
    block_spread = Spread(blocks, block_send, block_recv)
    loads[1].wait()
    right_spread.first()
    loads[2].wait()
    loads[3].wait()

    eye = lax.broadcasted_iota(I32, (FEAT, FEAT), 0) == lax.broadcasted_iota(I32, (FEAT, FEAT), 1)
    scale = jnp.sum(jnp.where(eye, inv_ref[...], 0.0), axis=1, keepdims=True)
    scaled = (pts_ref[...] * scale).astype(BF16).astype(F32)
    half_norm = jnp.sum(scaled * scaled, axis=0, keepdims=True) * -0.5
    cols_s[ROWS:, :] = jnp.zeros((128 - ROWS, HERE), F32)
    cols_s[0:FEAT, :] = scaled
    cols_s[FEAT:FEAT + 3, :] = jnp.ones((3, HERE), F32)
    for place, piece in enumerate(pieces(half_norm)):
        cols_s[FEAT + 3 + place:FEAT + 4 + place, :] = piece
    for part in range(HERE // 128):
        span = slice(part * 128, (part + 1) * 128)
        high, low = part // 2, (part % 2) * 128
        lookup[core, high, low:low + 128, :] = cols_s[:, span].T.astype(BF16)
    swap_lookup = remote(
        lookup.at[core], lookup.at[core], pair_send.at[0], pair_recv.at[0], pair
    )
    swap_lookup.start()
    loads[4].wait()
    swap_left = remote(lefts.at[0], lefts.at[1], pair_send.at[2], pair_recv.at[2], pair)
    swap_left.start()

    earlier = (
        lax.broadcasted_iota(I32, (BLK, BLK), 0) < lax.broadcasted_iota(I32, (BLK, BLK), 1)
    ).astype(F32).astype(BF16)

    own_owner = idx_all[chip] >> 12
    own_hits = jnp.where(
        lax.broadcasted_iota(I32, (CHIPS, BLK), 0) == own_owner, 1.0, 0.0
    )
    own_rank = jnp.dot(own_hits.astype(BF16), earlier, preferred_element_type=F32)
    own_rank = jnp.sum(own_rank * own_hits, axis=0, keepdims=True).astype(I32)

    loop(1, CHIPS, lambda m: idx_arrival(m).wait_recv())

    owner = jnp.concatenate([idx_all[d] for d in range(CHIPS)], axis=0) >> 12
    hits = jnp.where(owner == chip, 1.0, 0.0)
    rank = jnp.dot(hits.astype(BF16), earlier, preferred_element_type=F32)
    rank = jnp.where(hits > 0.5, rank, -1.0)
    for d in range(CHIPS):
        rank_all[d] = rank[d:d + 1, :]

    slot_row = lax.broadcasted_iota(I32, (SLOTS, BLK), 0).astype(F32)
    low_col = lax.broadcasted_iota(I32, (SLOTS, BLK), 1)

    def row_copy(turn, m):
        return remote(
            rows_out.at[turn, m], rows_in.at[turn, chip],
            row_send.at[turn, m], row_recv.at[turn, chip], {"pts": chip_at(m) * 2 + core},
        )

    def row_arrival(turn, m):
        there = chip_at(m)
        return remote(
            rows_out.at[turn, m], rows_in.at[turn, there],
            row_send.at[turn, m], row_recv.at[turn, there], {"pts": there * 2 + core},
        )

    groups = CHIPS // PER

    def each_round(act):
        for turn in range(rounds):
            loop(1, CHIPS, functools.partial(act, turn))

    swap_lookup.wait_recv()

    def look_up(step):
        turn, number = step // groups, lax.rem(step, groups)
        first_slot = (turn * SLOTS).astype(F32)
        picks, highs = [], []
        for u in range(PER):
            home = chip_at(number * PER + u)
            local = (idx_all[home] & (2 * HERE - 1)).astype(F32)
            chosen = rank_all[home] - first_slot == slot_row
            key = jnp.sum(jnp.where(chosen, local + 1.0, 0.0), axis=1, keepdims=True)
            key = key.astype(I32) - 1
            highs.append(key >> 8)
            picks.append(jnp.where((key & 255) == low_col, 1.0, 0.0).astype(BF16))
        pick = jnp.concatenate(picks, axis=0)
        high = jnp.concatenate(highs, axis=0)
        rows = jnp.zeros((PER * SLOTS, 128), F32)
        for half in range(2):
            table = jnp.concatenate([lookup[half, h] for h in range(8)], axis=1)
            found = jnp.dot(pick, table, preferred_element_type=F32)
            for h in range(8):
                rows = jnp.where(high == half * 8 + h, found[:, h * 128:(h + 1) * 128], rows)
        rows = rows.astype(BF16)
        for u in range(PER):
            rows_out[turn, number * PER + u] = rows[u * SLOTS:(u + 1) * SLOTS, :]
        for u in range(PER):
            m = number * PER + u

            @pl.when(m > 0)
            def _():
                row_copy(turn, m).start()

    loop(0, rounds * groups, look_up)
    for turn in range(rounds):
        rows_in[turn, chip] = rows_out[turn, 0]

    right_spread.second()

    slot = lax.broadcasted_iota(I32, (CHIPS * SLOTS, BLK), 0)
    placed = []
    for turn in range(rounds):
        spot = own_rank - turn * SLOTS
        spot = jnp.where((spot >= 0) & (spot < SLOTS), own_owner * SLOTS + spot, -1)
        placed.append(jnp.where(slot == spot, 1.0, 0.0).astype(BF16))

    def count(source, most):
        here = jnp.sum(jnp.where(owner == source, 1.0, 0.0), axis=1, keepdims=True)
        return jnp.maximum(most, here)

    most = lax.fori_loop(0, CHIPS, count, jnp.zeros((CHIPS, 1), F32))
    flag_mine[0] = jnp.broadcast_to(jnp.max(most, axis=0, keepdims=True), (8, 128))
    point_acc[...] = jnp.zeros_like(point_acc)

    each_round(lambda turn, m: row_arrival(turn, m).wait_recv())
    centres = jnp.zeros((128, BLK), F32)
    for turn in range(rounds):
        centres = centres + lax.dot_general(
            rows_in[turn].reshape(CHIPS * SLOTS, 128), placed[turn],
            (((0,), (0,)), ((), ())), preferred_element_type=F32,
        )
    here = slice(0, BLK)
    cols_s[0:ROWS, here] = centres[0:ROWS, :]
    norm_rows = cols_s[FEAT + 3:ROWS, here]
    cols_s[FEAT + 3:ROWS, here] = cols_s[FEAT:FEAT + 3, here]
    cols_s[FEAT:FEAT + 3, here] = norm_rows
    blocks[chip] = cols_s[0:ROWS, here].astype(BF16)

    block_spread.first()
    swap_left.wait_recv()

    def home_copy(m):
        return rail(to_home.at[m], at_home.at[m], home_send, home_recv.at[m], m)

    def multiply(numbers, last=None):
        blank = jnp.zeros((128 - ROWS, BLK), BF16)
        sides, mates = [], []
        for m in numbers:
            there = chip_at(m)
            cut = blocks[there]
            sides.append(jnp.concatenate([cut, blank], axis=0))
            mates.append(rights[there])
        side = sides[0] if len(sides) == 1 else jnp.concatenate(sides, axis=1)
        mate = mates[0] if len(mates) == 1 else jnp.concatenate(mates, axis=1)
        def tile(own, q, span):
            holder = core if own == 0 else 1 - core
            rows = jnp.concatenate([lookup[holder, 2 * q], lookup[holder, 2 * q + 1]], axis=0)
            power = jnp.dot(rows, side, preferred_element_type=F32) * LOG2E
            kernel = jnp.exp2(jnp.minimum(power, 0.0)).astype(BF16)
            point_acc[own, :, span] += lax.dot_general(
                mate, kernel, (((1,), (1,)), ((), ())), preferred_element_type=F32
            )
            return jnp.dot(lefts[own, :, span], kernel, preferred_element_type=F32)

        total = None
        for own in (1, 0):
            for t in range(4):
                if last:
                    part = tile(own, lax.rem(x + t + 1, 4), part_of(t + 1))
                else:
                    part = tile(own, t, slice(t * PART, (t + 1) * PART))
                total = part if total is None else total + part
                if last:
                    last(own, t)
        return total

    def part_of(step):
        return pl.ds(pl.multiple_of(lax.rem(x + step, 4) * PART, PART), PART)

    def swap_part(t):
        return remote(pair_out.at[t], pair_in.at[t], part_send.at[t], part_recv.at[t], pair)

    swap_flag = remote(flag_mine.at[0], flag_pair, pair_send.at[4], pair_recv.at[4], pair)

    def half_of(step, half):
        start = lax.rem(x + step, 4) * PART + half * HALF
        return pl.ds(pl.multiple_of(start, HALF), HALF)

    def x_copy(dx, half):
        return remote(
            x_out.at[dx - 1, half], x_in.at[dx - 1, half],
            x_send.at[dx - 1, half], x_recv.at[dx - 1, half], along_x(dx),
        )

    def chip_sum(dx, half):
        span = half_of(dx, half)
        arrived = pair_in[(dx + 3) % 4, :, half * HALF:(half + 1) * HALF]
        return point_acc[0, :, span] + arrived.astype(F32)

    def send_x(dx):
        for half in range(2):
            x_out[dx - 1, half] = chip_sum(dx, half).astype(BF16)
            x_copy(dx, half).start()

    def leave(own, t):
        if own == 1:
            pair_out[t] = point_acc[1, :, part_of(t + 1)].astype(BF16)
            swap_part(t).start()
        if (own, t) == (1, 3):
            swap_flag.start()
        if own == 0:
            swap_part(t).wait_recv()
        if own == 0 and t < 3:
            send_x(t + 1)

    own_part[...] = multiply([0])
    block_spread.second()

    def send_home(total, numbers):
        for u, m in enumerate(numbers):
            to_home[m] = total[:, u * BLK:(u + 1) * BLK].astype(BF16)
            home_copy(m).start()

    def arrive(numbers):
        for m in numbers:
            right_spread.arrive(m)
            block_spread.arrive(m)

    def advance(number):
        later = (number + 3) // 4
        numbers = [
            (1 - later) * (u + 1) + later * (number + 4 * (u + 1)) for u in range(3)
        ]

        @pl.when(number > 0)
        def _():
            arrive(numbers)

        send_home(multiply(numbers), numbers)

    loop(0, 4, advance)
    numbers = [4, 8, 12]
    arrive(numbers)
    send_home(multiply(numbers, leave), numbers)

    def flag_x_copy(dx):
        return remote(
            flag_mine.at[1], flag_x.at[dx - 1], fx_send.at[dx - 1], fx_recv.at[dx - 1], along_x(dx)
        )

    swap_flag.wait_recv()
    flag_mine[1] = jnp.maximum(flag_mine[0], flag_pair[...])
    for dx in (1, 2, 3):
        flag_x_copy(dx).start()

    worst = flag_mine[1]
    swap_z = [
        remote(z_out.at[half], z_in.at[half], z_send.at[half], z_recv.at[half], across)
        for half in range(2)
    ]
    for half in range(2):
        total = chip_sum(0, half)
        for dx in (1, 2, 3):
            x_copy(dx, half).wait_recv()
            total = total + x_in[dx - 1, half].astype(F32)
        z_out[half] = total.astype(BF16)
        swap_z[half].start()
    for dx in (1, 2, 3):
        flag_x_copy(dx).wait_recv()
        worst = jnp.maximum(worst, flag_x[dx - 1])
    flag_mine[2] = worst
    flag_across = remote(flag_mine.at[2], flag_z, z_send.at[2], z_recv.at[2], across)
    flag_across.start()

    loop(1, CHIPS, lambda m: home_copy(m).wait_recv())
    centre = own_part[...]
    for m in range(1, CHIPS):
        centre = centre + at_home[m].astype(F32)
    centre_ref[...] = centre

    def back_copy(dx, half):
        return remote(
            back_out.at[half], point_hbm.at[:, half_of(0, half)],
            back_send.at[dx - 1, half], back_recv.at[dx - 1, half], along_x(dx),
        )

    stores = []
    for half in range(2):
        swap_z[half].wait_recv()
        back_out[half] = (z_out[half].astype(F32) + z_in[half].astype(F32)).astype(BF16)
        for dx in (1, 2, 3):
            back_copy(dx, half).start()
        stores.append(pltpu.make_async_copy(
            back_out.at[half], point_hbm.at[:, half_of(0, half)], store_sem.at[half]
        ))
    flag_across.wait_recv()
    flag_ref[...] = jnp.maximum(flag_mine[2], flag_z[...])[0:1, 0:1]
    stores += [
        pltpu.make_async_copy(centre_ref, centre_hbm, store_sem.at[4]),
        pltpu.make_async_copy(flag_ref, flag_hbm, store_sem.at[5]),
    ]
    for store in stores:
        store.start()

    def drain(m):
        idx_copy(m).wait_send()
        right_spread.drain(m)
        block_spread.drain(m)
        home_copy(m).wait_send()

    loop(1, CHIPS, drain)
    each_round(lambda turn, m: row_copy(turn, m).wait_send())
    for copy in (swap_lookup, swap_left, swap_flag, *swap_z, flag_across):
        copy.wait_send()
    for t in range(4):
        swap_part(t).wait_send()
    for dx in (1, 2, 3):
        for half in range(2):
            x_copy(dx, half).wait_send()
        flag_x_copy(dx).wait_send()

    for half in range(2):
        for dx in (1, 2, 3):
            remote(
                back_out.at[half], point_hbm.at[:, half_of(4 - dx, half)],
                back_send.at[dx - 1, half], back_recv.at[dx - 1, half], along_x(dx),
            ).wait_recv()
            back_copy(dx, half).wait_send()
    for store in stores:
        store.wait()


def fused(rounds, points, centre_index, inv_scale, left_cols, right_cols):
    anywhere = pl.BlockSpec(memory_space=pl.ANY)
    dma = pltpu.SemaphoreType.DMA
    buf = pltpu.VMEM
    return pl.pallas_call(
        functools.partial(fused_kernel, rounds),
        out_shape=(
            jax.ShapeDtypeStruct((COLS, HERE), BF16),
            jax.ShapeDtypeStruct((COLS, BLK), F32),
            jax.ShapeDtypeStruct((1, 1), F32),
        ),
        in_specs=[anywhere] * 5,
        out_specs=[anywhere] * 3,
        scratch_shapes=[
            buf((FEAT, HERE), F32),
            buf((1, FEAT), F32),
            buf((COLS, BLK), F32),
            buf((1, 1), F32),
            dma((5,)),
            dma((6,)),
            buf((CHIPS, 1, BLK), I32),
            buf((CHIPS, 1, BLK), F32),
            buf((128, HERE), F32),
            buf((2, 8, 256, 128), BF16),
            buf((rounds, CHIPS, SLOTS, 128), BF16),
            buf((rounds, CHIPS, SLOTS, 128), BF16),
            buf((2, COLS, HERE), BF16),
            buf((CHIPS, ROWS, BLK), BF16),
            buf((CHIPS, COLS, BLK), BF16),
            buf((2, COLS, HERE), F32),
            buf((COLS, BLK), F32),
            buf((CHIPS, COLS, BLK), BF16),
            buf((CHIPS, COLS, BLK), BF16),
            buf((4, COLS, PART), BF16),
            buf((4, COLS, PART), BF16),
            buf((3, 2, COLS, HALF), BF16),
            buf((3, 2, COLS, HALF), BF16),
            buf((2, COLS, HALF), BF16),
            buf((2, COLS, HALF), BF16),
            buf((2, COLS, HALF), BF16),
            buf((3, 8, 128), F32),
            buf((8, 128), F32),
            buf((3, 8, 128), F32),
            buf((8, 128), F32),
        ]
        + [dma((CHIPS,))] * 2
        + [dma((rounds, CHIPS))] * 2
        + [dma((CHIPS,))] * 6
        + [dma((5,)), dma((5,)), dma((4,)), dma((4,)), dma((3, 2)), dma((3, 2)), dma((3,)), dma((3,))]
        + [dma((3, 2))] * 2
        + [dma((3,))] * 2,
        compiler_params=pltpu.CompilerParams(
            collective_id=rounds, has_side_effects=True, vmem_limit_bytes=VMEM_LIMIT
        ),
        name=f"nystrom_products_{rounds}",
    )(points, inv_scale[None, :], centre_index[None, :], left_cols, right_cols)


ROUNDS = -(-BLK // SLOTS)


def body(*arguments):
    point_side, centre_side, most = fused(1, *arguments)
    point_side, centre_side = lax.cond(
        most[0, 0] > SLOTS, lambda: fused(ROUNDS, *arguments)[:2], lambda: (point_side, centre_side)
    )
    return point_side.astype(F32), centre_side


def solution(mesh):
    return jax.shard_map(
        body,
        mesh=mesh,
        in_specs=(P(None, "pts"), P(("ctr", "pts")), P(), P(None, "pts"), P(None, ("ctr", "pts"))),
        out_specs=(P(None, "pts"), P(None, ("ctr", "pts"))),
        check_vma=False,
    )
```

```python
import functools
import math

import jax
import jax.numpy as jnp
from jax import lax
from jax.experimental import pallas as pl
from jax.experimental.pallas import tpu as pltpu
from jax.sharding import PartitionSpec as P

F32, BF16, I32 = jnp.float32, jnp.bfloat16, jnp.int32
MESH = pl.DeviceIdType.MESH
LOG2E = math.log2(math.e)
FEAT = 90
ROWS = 96
COLS = 64
HERE = 2048
BLK = 256
CHIPS = 16
SLOTS = 48
PER = 8
PART = HERE // 4
HALF = PART // 2
VMEM_LIMIT = 56 * 2**20


def pieces(value):
    first = value.astype(BF16).astype(F32)
    second = (value - first).astype(BF16).astype(F32)
    third = (value - first - second).astype(BF16).astype(F32)
    return first, second, third


def fused_kernel(
    rounds, pts_hbm, inv_hbm, idx_hbm, left_hbm, right_hbm,
    point_hbm, centre_hbm, flag_hbm,
    pts_ref, inv_ref, centre_ref, flag_ref, load_sem, store_sem,
    idx_all, rank_all, cols_s, lookup, rows_out, rows_in,
    lefts, blocks, rights, point_acc, own_part, to_home, at_home,
    pair_out, pair_in, x_out, x_in, z_out, z_in, back_out,
    flag_mine, flag_pair, flag_x, flag_z,
    idx_send, idx_recv, row_send, row_recv, right_send, right_recv,
    block_send, block_recv, home_send, home_recv, pair_send, pair_recv,
    part_send, part_recv, x_send, x_recv, z_send, z_recv, back_send, back_recv, fx_send, fx_recv,
):
    me = lax.axis_index("pts")
    panel = lax.axis_index("ctr")
    chip, core = me // 2, lax.rem(me, 2)
    z, y = chip // 4, lax.rem(chip, 4)
    x, z_hi = panel // 2, lax.rem(panel, 2)
    pair = {"pts": chip * 2 + 1 - core}
    across = {"ctr": x * 2 + 1 - z_hi}

    def chip_at(m):
        return lax.rem(z + lax.rem(m, 4), 4) * 4 + lax.rem(y + m // 4, 4)

    def along_x(dx):
        return {"ctr": lax.rem(x + dx, 4) * 2 + z_hi}

    def remote(src, dst, send, recv, device):
        return pltpu.make_async_remote_copy(
            src_ref=src, dst_ref=dst, send_sem=send, recv_sem=recv,
            device_id=device, device_id_type=MESH,
        )

    def loop(first, last, act):
        def step(m, _):
            act(m)
            return 0

        lax.fori_loop(first, last, step, 0)

    loads = [
        pltpu.make_async_copy(source, here, load_sem.at[number])
        for number, (source, here) in enumerate((
            (idx_hbm, idx_all.at[chip]), (right_hbm, rights.at[chip]), (pts_hbm, pts_ref),
            (inv_hbm, inv_ref), (left_hbm, lefts.at[0]),
        ))
    ]
    for load in loads:
        load.start()

    barrier = pltpu.get_barrier_semaphore()
    pl.semaphore_signal(barrier, inc=1, device_id=across, device_id_type=MESH)
    for dx in (1, 2, 3):
        pl.semaphore_signal(barrier, inc=1, device_id=along_x(dx), device_id_type=MESH)
    loop(1, CHIPS, lambda m: pl.semaphore_signal(
        barrier, inc=1, device_id={"pts": chip_at(m) * 2 + core}, device_id_type=MESH
    ))
    pl.semaphore_signal(barrier, inc=1, device_id=pair, device_id_type=MESH)
    pl.semaphore_wait(barrier, CHIPS + 4)

    def rail(src, dst, send, recv, m):
        return remote(src, dst, send.at[m], recv, {"pts": chip_at(m) * 2 + core})

    def idx_copy(m):
        return rail(idx_all.at[chip], idx_all.at[chip], idx_send, idx_recv.at[chip], m)

    def idx_arrival(m):
        there = chip_at(m)
        return rail(idx_all.at[chip], idx_all.at[there], idx_send, idx_recv.at[there], m)

    loads[0].wait()
    loop(1, CHIPS, lambda m: idx_copy(m).start())

    class Spread:
        def __init__(self, held, send, recv):
            self.held, self.send, self.recv = held, send, recv

        def copy(self, m, source):
            there = chip_at(source)
            return rail(self.held.at[there], self.held.at[there], self.send, self.recv.at[there], m)

        def first(self):
            for d in (1, 2, 3):
                self.copy(d, 0).start()
            for d in (1, 2, 3):
                self.copy(4 * d, 0).start()

        def second(self):
            for dz in (1, 2, 3):
                self.arrive(dz)
                for dy in (1, 2, 3):
                    rail_on = {"pts": chip_at(4 * dy) * 2 + core}
                    there = chip_at(dz)
                    remote(
                        self.held.at[there], self.held.at[there],
                        self.send.at[dz + 4 * dy], self.recv.at[there], rail_on,
                    ).start()

        def arrive(self, m):
            self.copy(m, m).wait_recv()

        def drain(self, m):
            self.copy(m, 0).wait_send()

    right_spread = Spread(rights, right_send, right_recv)
    block_spread = Spread(blocks, block_send, block_recv)
    loads[1].wait()
    right_spread.first()
    loads[2].wait()
    loads[3].wait()

    eye = lax.broadcasted_iota(I32, (FEAT, FEAT), 0) == lax.broadcasted_iota(I32, (FEAT, FEAT), 1)
    scale = jnp.sum(jnp.where(eye, inv_ref[...], 0.0), axis=1, keepdims=True)
    scaled = (pts_ref[...] * scale).astype(BF16).astype(F32)
    half_norm = jnp.sum(scaled * scaled, axis=0, keepdims=True) * -0.5
    cols_s[ROWS:, :] = jnp.zeros((128 - ROWS, HERE), F32)
    cols_s[0:FEAT, :] = scaled
    cols_s[FEAT:FEAT + 3, :] = jnp.ones((3, HERE), F32)
    for place, piece in enumerate(pieces(half_norm)):
        cols_s[FEAT + 3 + place:FEAT + 4 + place, :] = piece
    for part in range(HERE // 128):
        span = slice(part * 128, (part + 1) * 128)
        high, low = part // 2, (part % 2) * 128
        lookup[core, high, low:low + 128, :] = cols_s[:, span].T.astype(BF16)
    swap_lookup = remote(
        lookup.at[core], lookup.at[core], pair_send.at[0], pair_recv.at[0], pair
    )
    swap_lookup.start()
    loads[4].wait()
    swap_left = remote(lefts.at[0], lefts.at[1], pair_send.at[2], pair_recv.at[2], pair)
    swap_left.start()

    earlier = (
        lax.broadcasted_iota(I32, (BLK, BLK), 0) < lax.broadcasted_iota(I32, (BLK, BLK), 1)
    ).astype(F32).astype(BF16)

    own_owner = idx_all[chip] >> 12
    own_hits = jnp.where(
        lax.broadcasted_iota(I32, (CHIPS, BLK), 0) == own_owner, 1.0, 0.0
    )
    own_rank = jnp.dot(own_hits.astype(BF16), earlier, preferred_element_type=F32)
    own_rank = jnp.sum(own_rank * own_hits, axis=0, keepdims=True).astype(I32)

    loop(1, CHIPS, lambda m: idx_arrival(m).wait_recv())

    owner = jnp.concatenate([idx_all[d] for d in range(CHIPS)], axis=0) >> 12
    hits = jnp.where(owner == chip, 1.0, 0.0)
    rank = jnp.dot(hits.astype(BF16), earlier, preferred_element_type=F32)
    rank = jnp.where(hits > 0.5, rank, -1.0)
    for d in range(CHIPS):
        rank_all[d] = rank[d:d + 1, :]

    slot_row = lax.broadcasted_iota(I32, (SLOTS, BLK), 0).astype(F32)
    low_col = lax.broadcasted_iota(I32, (SLOTS, BLK), 1)

    def row_copy(turn, m):
        return remote(
            rows_out.at[turn, m], rows_in.at[turn, chip],
            row_send.at[turn, m], row_recv.at[turn, chip], {"pts": chip_at(m) * 2 + core},
        )

    def row_arrival(turn, m):
        there = chip_at(m)
        return remote(
            rows_out.at[turn, m], rows_in.at[turn, there],
            row_send.at[turn, m], row_recv.at[turn, there], {"pts": there * 2 + core},
        )

    groups = CHIPS // PER

    def each_round(act):
        for turn in range(rounds):
            loop(1, CHIPS, functools.partial(act, turn))

    swap_lookup.wait_recv()

    def look_up(step):
        turn, number = step // groups, lax.rem(step, groups)
        first_slot = (turn * SLOTS).astype(F32)
        picks, highs = [], []
        for u in range(PER):
            home = chip_at(number * PER + u)
            local = (idx_all[home] & (2 * HERE - 1)).astype(F32)
            chosen = rank_all[home] - first_slot == slot_row
            key = jnp.sum(jnp.where(chosen, local + 1.0, 0.0), axis=1, keepdims=True)
            key = key.astype(I32) - 1
            highs.append(key >> 8)
            picks.append(jnp.where((key & 255) == low_col, 1.0, 0.0).astype(BF16))
        pick = jnp.concatenate(picks, axis=0)
        high = jnp.concatenate(highs, axis=0)
        rows = jnp.zeros((PER * SLOTS, 128), F32)
        for half in range(2):
            table = jnp.concatenate([lookup[half, h] for h in range(8)], axis=1)
            found = jnp.dot(pick, table, preferred_element_type=F32)
            for h in range(8):
                rows = jnp.where(high == half * 8 + h, found[:, h * 128:(h + 1) * 128], rows)
        rows = rows.astype(BF16)
        for u in range(PER):
            rows_out[turn, number * PER + u] = rows[u * SLOTS:(u + 1) * SLOTS, :]
        for u in range(PER):
            m = number * PER + u

            @pl.when(m > 0)
            def _():
                row_copy(turn, m).start()

    loop(0, rounds * groups, look_up)
    for turn in range(rounds):
        rows_in[turn, chip] = rows_out[turn, 0]

    right_spread.second()

    slot = lax.broadcasted_iota(I32, (CHIPS * SLOTS, BLK), 0)
    placed = []
    for turn in range(rounds):
        spot = own_rank - turn * SLOTS
        spot = jnp.where((spot >= 0) & (spot < SLOTS), own_owner * SLOTS + spot, -1)
        placed.append(jnp.where(slot == spot, 1.0, 0.0).astype(BF16))

    def count(source, most):
        here = jnp.sum(jnp.where(owner == source, 1.0, 0.0), axis=1, keepdims=True)
        return jnp.maximum(most, here)

    most = lax.fori_loop(0, CHIPS, count, jnp.zeros((CHIPS, 1), F32))
    flag_mine[0] = jnp.broadcast_to(jnp.max(most, axis=0, keepdims=True), (8, 128))
    point_acc[...] = jnp.zeros_like(point_acc)

    each_round(lambda turn, m: row_arrival(turn, m).wait_recv())
    centres = jnp.zeros((128, BLK), F32)
    for turn in range(rounds):
        centres = centres + lax.dot_general(
            rows_in[turn].reshape(CHIPS * SLOTS, 128), placed[turn],
            (((0,), (0,)), ((), ())), preferred_element_type=F32,
        )
    here = slice(0, BLK)
    cols_s[0:ROWS, here] = centres[0:ROWS, :]
    norm_rows = cols_s[FEAT + 3:ROWS, here]
    cols_s[FEAT + 3:ROWS, here] = cols_s[FEAT:FEAT + 3, here]
    cols_s[FEAT:FEAT + 3, here] = norm_rows
    blocks[chip] = cols_s[0:ROWS, here].astype(BF16)

    block_spread.first()
    swap_left.wait_recv()

    def home_copy(m):
        return rail(to_home.at[m], at_home.at[m], home_send, home_recv.at[m], m)

    def send_home(total, numbers):
        if numbers == [0]:
            own_part[...] = total
            return
        for u, m in enumerate(numbers):
            to_home[m] = total[:, u * BLK:(u + 1) * BLK].astype(BF16)
            home_copy(m).start()

    plain = [(0, own, t) for own in (1, 0) for t in range(4)]

    def multiply(sets, order=plain, after=None):
        blank = jnp.zeros((128 - ROWS, BLK), BF16)
        sides, mates = [], []
        for numbers in sets:
            places = [chip_at(m) for m in numbers]
            sides.append(jnp.concatenate(
                [jnp.concatenate([blocks[there], blank], axis=0) for there in places], axis=1
            ))
            mates.append(jnp.concatenate([rights[there] for there in places], axis=1))

        def tile(own, q, span, side, mate):
            holder = core if own == 0 else 1 - core
            rows = jnp.concatenate([lookup[holder, 2 * q], lookup[holder, 2 * q + 1]], axis=0)
            power = jnp.dot(rows, side, preferred_element_type=F32) * LOG2E
            kernel = jnp.exp2(jnp.minimum(power, 0.0)).astype(BF16)
            point_acc[own, :, span] += lax.dot_general(
                mate, kernel, (((1,), (1,)), ((), ())), preferred_element_type=F32
            )
            return jnp.dot(lefts[own, :, span], kernel, preferred_element_type=F32)

        totals = [None for _ in sets]
        for place, (number, own, t) in enumerate(order):
            if after:
                q, span = lax.rem(x + t + 1, 4), part_of(t + 1)
            else:
                q, span = t, slice(t * PART, (t + 1) * PART)
            part = tile(own, q, span, sides[number], mates[number])
            total = totals[number]
            totals[number] = part if total is None else total + part
            if number not in [later[0] for later in order[place + 1:]]:
                send_home(totals[number], sets[number])
            if after:
                after(number, own, t)
        return totals

    def part_of(step):
        return pl.ds(pl.multiple_of(lax.rem(x + step, 4) * PART, PART), PART)

    def swap_part(t):
        return remote(pair_out.at[t], pair_in.at[t], part_send.at[t], part_recv.at[t], pair)

    swap_flag = remote(flag_mine.at[0], flag_pair, pair_send.at[4], pair_recv.at[4], pair)

    def half_of(step, half):
        start = lax.rem(x + step, 4) * PART + half * HALF
        return pl.ds(pl.multiple_of(start, HALF), HALF)

    def x_copy(dx, half):
        return remote(
            x_out.at[dx - 1, half], x_in.at[dx - 1, half],
            x_send.at[dx - 1, half], x_recv.at[dx - 1, half], along_x(dx),
        )

    def chip_sum(dx, half):
        span = half_of(dx, half)
        arrived = pair_in[(dx + 3) % 4, :, half * HALF:(half + 1) * HALF]
        return point_acc[0, :, span] + arrived.astype(F32)

    def send_x(dx):
        for half in range(2):
            x_out[dx - 1, half] = chip_sum(dx, half).astype(BF16)
            x_copy(dx, half).start()

    def leave(number, own, t):
        if own == 1:
            pair_out[t] = point_acc[1, :, part_of(t + 1)].astype(BF16)
            swap_part(t).start()
        if (own, t) == (1, 0):
            swap_flag.start()
        if own == 0 and t < 3:
            swap_part(t).wait_recv()
            send_x(t + 1)

    multiply([[0]])
    block_spread.second()

    def arrive(numbers):
        for m in numbers:
            right_spread.arrive(m)
            block_spread.arrive(m)

    def advance(number):
        later = (number + 3) // 4
        numbers = [
            (1 - later) * (u + 1) + later * (number + 4 * (u + 1)) for u in range(3)
        ]

        @pl.when(number > 0)
        def _():
            arrive(numbers)

        multiply([numbers])

    loop(0, 4, advance)
    numbers = [4, 8, 12]
    arrive(numbers)
    order = [(0, own, t) for own in (1, 0) for t in range(3)] + [(0, 1, 3), (0, 0, 3)]
    multiply([numbers], order, leave)

    def flag_x_copy(dx):
        return remote(
            flag_mine.at[1], flag_x.at[dx - 1], fx_send.at[dx - 1], fx_recv.at[dx - 1], along_x(dx)
        )

    swap_flag.wait_recv()
    flag_mine[1] = jnp.maximum(flag_mine[0], flag_pair[...])
    for dx in (1, 2, 3):
        flag_x_copy(dx).start()

    swap_part(3).wait_recv()
    worst = flag_mine[1]
    swap_z = [
        remote(z_out.at[half], z_in.at[half], z_send.at[half], z_recv.at[half], across)
        for half in range(2)
    ]
    for half in range(2):
        total = chip_sum(0, half)
        for dx in (1, 2, 3):
            x_copy(dx, half).wait_recv()
            total = total + x_in[dx - 1, half].astype(F32)
        z_out[half] = total.astype(BF16)
        swap_z[half].start()
    for dx in (1, 2, 3):
        flag_x_copy(dx).wait_recv()
        worst = jnp.maximum(worst, flag_x[dx - 1])
    flag_mine[2] = worst
    flag_across = remote(flag_mine.at[2], flag_z, z_send.at[2], z_recv.at[2], across)
    flag_across.start()

    def back_copy(dx, half):
        return remote(
            back_out.at[half], point_hbm.at[:, half_of(0, half)],
            back_send.at[dx - 1, half], back_recv.at[dx - 1, half], along_x(dx),
        )

    stores = []
    for half in range(2):
        swap_z[half].wait_recv()
        back_out[half] = (z_out[half].astype(F32) + z_in[half].astype(F32)).astype(BF16)
        for dx in (1, 2, 3):
            back_copy(dx, half).start()
        stores.append(pltpu.make_async_copy(
            back_out.at[half], point_hbm.at[:, half_of(0, half)], store_sem.at[half]
        ))
    loop(1, CHIPS, lambda m: home_copy(m).wait_recv())
    centre = own_part[...]
    for m in range(1, CHIPS):
        centre = centre + at_home[m].astype(F32)
    centre_ref[...] = centre

    flag_across.wait_recv()
    flag_ref[...] = jnp.maximum(flag_mine[2], flag_z[...])[0:1, 0:1]
    stores += [
        pltpu.make_async_copy(centre_ref, centre_hbm, store_sem.at[4]),
        pltpu.make_async_copy(flag_ref, flag_hbm, store_sem.at[5]),
    ]
    for store in stores:
        store.start()

    def drain(m):
        idx_copy(m).wait_send()
        right_spread.drain(m)
        block_spread.drain(m)
        home_copy(m).wait_send()

    loop(1, CHIPS, drain)
    each_round(lambda turn, m: row_copy(turn, m).wait_send())
    for copy in (swap_lookup, swap_left, swap_flag, *swap_z, flag_across):
        copy.wait_send()
    for t in range(4):
        swap_part(t).wait_send()
    for dx in (1, 2, 3):
        for half in range(2):
            x_copy(dx, half).wait_send()
        flag_x_copy(dx).wait_send()

    for half in range(2):
        for dx in (1, 2, 3):
            remote(
                back_out.at[half], point_hbm.at[:, half_of(4 - dx, half)],
                back_send.at[dx - 1, half], back_recv.at[dx - 1, half], along_x(dx),
            ).wait_recv()
            back_copy(dx, half).wait_send()
    for store in stores:
        store.wait()


def fused(rounds, points, centre_index, inv_scale, left_cols, right_cols):
    anywhere = pl.BlockSpec(memory_space=pl.ANY)
    dma = pltpu.SemaphoreType.DMA
    buf = pltpu.VMEM
    return pl.pallas_call(
        functools.partial(fused_kernel, rounds),
        out_shape=(
            jax.ShapeDtypeStruct((COLS, HERE), BF16),
            jax.ShapeDtypeStruct((COLS, BLK), F32),
            jax.ShapeDtypeStruct((1, 1), F32),
        ),
        in_specs=[anywhere] * 5,
        out_specs=[anywhere] * 3,
        scratch_shapes=[
            buf((FEAT, HERE), F32),
            buf((1, FEAT), F32),
            buf((COLS, BLK), F32),
            buf((1, 1), F32),
            dma((5,)),
            dma((6,)),
            buf((CHIPS, 1, BLK), I32),
            buf((CHIPS, 1, BLK), F32),
            buf((128, HERE), F32),
            buf((2, 8, 256, 128), BF16),
            buf((rounds, CHIPS, SLOTS, 128), BF16),
            buf((rounds, CHIPS, SLOTS, 128), BF16),
            buf((2, COLS, HERE), BF16),
            buf((CHIPS, ROWS, BLK), BF16),
            buf((CHIPS, COLS, BLK), BF16),
            buf((2, COLS, HERE), F32),
            buf((COLS, BLK), F32),
            buf((CHIPS, COLS, BLK), BF16),
            buf((CHIPS, COLS, BLK), BF16),
            buf((4, COLS, PART), BF16),
            buf((4, COLS, PART), BF16),
            buf((3, 2, COLS, HALF), BF16),
            buf((3, 2, COLS, HALF), BF16),
            buf((2, COLS, HALF), BF16),
            buf((2, COLS, HALF), BF16),
            buf((2, COLS, HALF), BF16),
            buf((3, 8, 128), F32),
            buf((8, 128), F32),
            buf((3, 8, 128), F32),
            buf((8, 128), F32),
        ]
        + [dma((CHIPS,))] * 2
        + [dma((rounds, CHIPS))] * 2
        + [dma((CHIPS,))] * 6
        + [dma((5,)), dma((5,)), dma((4,)), dma((4,)), dma((3, 2)), dma((3, 2)), dma((3,)), dma((3,))]
        + [dma((3, 2))] * 2
        + [dma((3,))] * 2,
        compiler_params=pltpu.CompilerParams(
            collective_id=rounds, has_side_effects=True, vmem_limit_bytes=VMEM_LIMIT
        ),
        name=f"nystrom_products_{rounds}",
    )(points, inv_scale[None, :], centre_index[None, :], left_cols, right_cols)


ROUNDS = -(-BLK // SLOTS)


def body(*arguments):
    point_side, centre_side, most = fused(1, *arguments)
    point_side, centre_side = lax.cond(
        most[0, 0] > SLOTS, lambda: fused(ROUNDS, *arguments)[:2], lambda: (point_side, centre_side)
    )
    return point_side.astype(F32), centre_side


def solution(mesh):
    return jax.shard_map(
        body,
        mesh=mesh,
        in_specs=(P(None, "pts"), P(("ctr", "pts")), P(), P(None, "pts"), P(None, ("ctr", "pts"))),
        out_specs=(P(None, "pts"), P(None, ("ctr", "pts"))),
        check_vma=False,
    )
```

```python
import functools
import math

import jax
import jax.numpy as jnp
from jax import lax
from jax.experimental import pallas as pl
from jax.experimental.pallas import tpu as pltpu
from jax.sharding import PartitionSpec as P

F32, BF16, I32 = jnp.float32, jnp.bfloat16, jnp.int32
MESH = pl.DeviceIdType.MESH
LOG2E = math.log2(math.e)
FEAT = 90
ROWS = 96
COLS = 64
HERE = 2048
BLK = 256
CHIPS = 16
SLOTS = 48
PER = 8
PART = HERE // 4
HALF = PART // 2
VMEM_LIMIT = 56 * 2**20


def pieces(value):
    first = value.astype(BF16).astype(F32)
    second = (value - first).astype(BF16).astype(F32)
    third = (value - first - second).astype(BF16).astype(F32)
    return first, second, third


def fused_kernel(
    rounds, pts_hbm, inv_hbm, idx_hbm, left_hbm, right_hbm,
    point_hbm, centre_hbm, flag_hbm,
    pts_ref, inv_ref, centre_ref, flag_ref, load_sem, store_sem,
    idx_all, rank_all, cols_s, lookup, rows_out, rows_in,
    lefts, blocks, rights, point_acc, own_part, to_home, at_home,
    pair_out, pair_in, x_out, x_in, z_out, z_in, back_out,
    flag_mine, flag_pair, flag_x, flag_z,
    idx_send, idx_recv, row_send, row_recv, right_send, right_recv,
    block_send, block_recv, home_send, home_recv, pair_send, pair_recv,
    part_send, part_recv, x_send, x_recv, z_send, z_recv, back_send, back_recv, fx_send, fx_recv,
):
    me = lax.axis_index("pts")
    panel = lax.axis_index("ctr")
    chip, core = me // 2, lax.rem(me, 2)
    z, y = chip // 4, lax.rem(chip, 4)
    x, z_hi = panel // 2, lax.rem(panel, 2)
    pair = {"pts": chip * 2 + 1 - core}
    across = {"ctr": x * 2 + 1 - z_hi}

    def chip_at(m):
        return lax.rem(z + lax.rem(m, 4), 4) * 4 + lax.rem(y + m // 4, 4)

    def along_x(dx):
        return {"ctr": lax.rem(x + dx, 4) * 2 + z_hi}

    def remote(src, dst, send, recv, device):
        return pltpu.make_async_remote_copy(
            src_ref=src, dst_ref=dst, send_sem=send, recv_sem=recv,
            device_id=device, device_id_type=MESH,
        )

    def loop(first, last, act):
        def step(m, _):
            act(m)
            return 0

        lax.fori_loop(first, last, step, 0)

    loads = [
        pltpu.make_async_copy(source, here, load_sem.at[number])
        for number, (source, here) in enumerate((
            (idx_hbm, idx_all.at[chip]), (right_hbm, rights.at[chip]), (pts_hbm, pts_ref),
            (inv_hbm, inv_ref), (left_hbm, lefts.at[0]),
        ))
    ]
    for load in loads:
        load.start()

    barrier = pltpu.get_barrier_semaphore()
    pl.semaphore_signal(barrier, inc=1, device_id=across, device_id_type=MESH)
    for dx in (1, 2, 3):
        pl.semaphore_signal(barrier, inc=1, device_id=along_x(dx), device_id_type=MESH)
    loop(1, CHIPS, lambda m: pl.semaphore_signal(
        barrier, inc=1, device_id={"pts": chip_at(m) * 2 + core}, device_id_type=MESH
    ))
    pl.semaphore_signal(barrier, inc=1, device_id=pair, device_id_type=MESH)
    pl.semaphore_wait(barrier, CHIPS + 4)

    def rail(src, dst, send, recv, m):
        return remote(src, dst, send.at[m], recv, {"pts": chip_at(m) * 2 + core})

    def idx_copy(m):
        return rail(idx_all.at[chip], idx_all.at[chip], idx_send, idx_recv.at[chip], m)

    def idx_arrival(m):
        there = chip_at(m)
        return rail(idx_all.at[chip], idx_all.at[there], idx_send, idx_recv.at[there], m)

    loads[0].wait()
    loop(1, CHIPS, lambda m: idx_copy(m).start())

    class Spread:
        def __init__(self, held, send, recv):
            self.held, self.send, self.recv = held, send, recv

        def copy(self, m, source):
            there = chip_at(source)
            return rail(self.held.at[there], self.held.at[there], self.send, self.recv.at[there], m)

        def first(self):
            for d in (1, 2, 3):
                self.copy(d, 0).start()
            for d in (1, 2, 3):
                self.copy(4 * d, 0).start()

        def second(self):
            for dz in (1, 2, 3):
                self.arrive(dz)
                for dy in (1, 2, 3):
                    rail_on = {"pts": chip_at(4 * dy) * 2 + core}
                    there = chip_at(dz)
                    remote(
                        self.held.at[there], self.held.at[there],
                        self.send.at[dz + 4 * dy], self.recv.at[there], rail_on,
                    ).start()

        def arrive(self, m):
            self.copy(m, m).wait_recv()

        def drain(self, m):
            self.copy(m, 0).wait_send()

    right_spread = Spread(rights, right_send, right_recv)
    block_spread = Spread(blocks, block_send, block_recv)
    loads[1].wait()
    right_spread.first()
    loads[2].wait()
    loads[3].wait()

    eye = lax.broadcasted_iota(I32, (FEAT, FEAT), 0) == lax.broadcasted_iota(I32, (FEAT, FEAT), 1)
    scale = jnp.sum(jnp.where(eye, inv_ref[...], 0.0), axis=1, keepdims=True)
    scaled = (pts_ref[...] * scale).astype(BF16).astype(F32)
    half_norm = jnp.sum(scaled * scaled, axis=0, keepdims=True) * -0.5
    cols_s[ROWS:, :] = jnp.zeros((128 - ROWS, HERE), F32)
    cols_s[0:FEAT, :] = scaled
    cols_s[FEAT:FEAT + 3, :] = jnp.ones((3, HERE), F32)
    for place, piece in enumerate(pieces(half_norm)):
        cols_s[FEAT + 3 + place:FEAT + 4 + place, :] = piece
    for part in range(HERE // 128):
        span = slice(part * 128, (part + 1) * 128)
        high, low = part // 2, (part % 2) * 128
        lookup[core, high, low:low + 128, :] = cols_s[:, span].T.astype(BF16)
    swap_lookup = remote(
        lookup.at[core], lookup.at[core], pair_send.at[0], pair_recv.at[0], pair
    )
    swap_lookup.start()
    loads[4].wait()
    swap_left = remote(lefts.at[0], lefts.at[1], pair_send.at[2], pair_recv.at[2], pair)
    swap_left.start()

    earlier = (
        lax.broadcasted_iota(I32, (BLK, BLK), 0) < lax.broadcasted_iota(I32, (BLK, BLK), 1)
    ).astype(F32).astype(BF16)

    own_owner = idx_all[chip] >> 12
    own_hits = jnp.where(
        lax.broadcasted_iota(I32, (CHIPS, BLK), 0) == own_owner, 1.0, 0.0
    )
    own_rank = jnp.dot(own_hits.astype(BF16), earlier, preferred_element_type=F32)
    own_rank = jnp.sum(own_rank * own_hits, axis=0, keepdims=True).astype(I32)

    loop(1, CHIPS, lambda m: idx_arrival(m).wait_recv())

    owner = jnp.concatenate([idx_all[d] for d in range(CHIPS)], axis=0) >> 12
    hits = jnp.where(owner == chip, 1.0, 0.0)
    rank = jnp.dot(hits.astype(BF16), earlier, preferred_element_type=F32)
    rank = jnp.where(hits > 0.5, rank, -1.0)
    for d in range(CHIPS):
        rank_all[d] = rank[d:d + 1, :]

    slot_row = lax.broadcasted_iota(I32, (SLOTS, BLK), 0).astype(F32)
    low_col = lax.broadcasted_iota(I32, (SLOTS, BLK), 1)

    def row_copy(turn, m):
        return remote(
            rows_out.at[turn, m], rows_in.at[turn, chip],
            row_send.at[turn, m], row_recv.at[turn, chip], {"pts": chip_at(m) * 2 + core},
        )

    def row_arrival(turn, m):
        there = chip_at(m)
        return remote(
            rows_out.at[turn, m], rows_in.at[turn, there],
            row_send.at[turn, m], row_recv.at[turn, there], {"pts": there * 2 + core},
        )

    groups = CHIPS // PER

    def each_round(act):
        for turn in range(rounds):
            loop(1, CHIPS, functools.partial(act, turn))

    swap_lookup.wait_recv()

    def look_up(step):
        turn, number = step // groups, lax.rem(step, groups)
        first_slot = (turn * SLOTS).astype(F32)
        picks, highs = [], []
        for u in range(PER):
            home = chip_at(number * PER + u)
            local = (idx_all[home] & (2 * HERE - 1)).astype(F32)
            chosen = rank_all[home] - first_slot == slot_row
            key = jnp.sum(jnp.where(chosen, local + 1.0, 0.0), axis=1, keepdims=True)
            key = key.astype(I32) - 1
            highs.append(key >> 8)
            picks.append(jnp.where((key & 255) == low_col, 1.0, 0.0).astype(BF16))
        pick = jnp.concatenate(picks, axis=0)
        high = jnp.concatenate(highs, axis=0)
        rows = jnp.zeros((PER * SLOTS, 128), F32)
        for half in range(2):
            table = jnp.concatenate([lookup[half, h] for h in range(8)], axis=1)
            found = jnp.dot(pick, table, preferred_element_type=F32)
            for h in range(8):
                rows = jnp.where(high == half * 8 + h, found[:, h * 128:(h + 1) * 128], rows)
        rows = rows.astype(BF16)
        for u in range(PER):
            rows_out[turn, number * PER + u] = rows[u * SLOTS:(u + 1) * SLOTS, :]
        for u in range(PER):
            m = number * PER + u

            @pl.when(m > 0)
            def _():
                row_copy(turn, m).start()

    loop(0, rounds * groups, look_up)
    for turn in range(rounds):
        rows_in[turn, chip] = rows_out[turn, 0]

    right_spread.second()

    slot = lax.broadcasted_iota(I32, (CHIPS * SLOTS, BLK), 0)
    placed = []
    for turn in range(rounds):
        spot = own_rank - turn * SLOTS
        spot = jnp.where((spot >= 0) & (spot < SLOTS), own_owner * SLOTS + spot, -1)
        placed.append(jnp.where(slot == spot, 1.0, 0.0).astype(BF16))

    def count(source, most):
        here = jnp.sum(jnp.where(owner == source, 1.0, 0.0), axis=1, keepdims=True)
        return jnp.maximum(most, here)

    most = lax.fori_loop(0, CHIPS, count, jnp.zeros((CHIPS, 1), F32))
    flag_mine[0] = jnp.broadcast_to(jnp.max(most, axis=0, keepdims=True), (8, 128))
    point_acc[...] = jnp.zeros_like(point_acc)

    each_round(lambda turn, m: row_arrival(turn, m).wait_recv())
    centres = jnp.zeros((128, BLK), F32)
    for turn in range(rounds):
        centres = centres + lax.dot_general(
            rows_in[turn].reshape(CHIPS * SLOTS, 128), placed[turn],
            (((0,), (0,)), ((), ())), preferred_element_type=F32,
        )
    here = slice(0, BLK)
    cols_s[0:ROWS, here] = centres[0:ROWS, :]
    norm_rows = cols_s[FEAT + 3:ROWS, here]
    cols_s[FEAT + 3:ROWS, here] = cols_s[FEAT:FEAT + 3, here]
    cols_s[FEAT:FEAT + 3, here] = norm_rows
    blocks[chip] = cols_s[0:ROWS, here].astype(BF16)

    block_spread.first()
    swap_left.wait_recv()

    def home_copy(m):
        return rail(to_home.at[m], at_home.at[m], home_send, home_recv.at[m], m)

    def send_home(total, numbers):
        if numbers == [0]:
            own_part[...] = total
            return
        for u, m in enumerate(numbers):
            to_home[m] = total[:, u * BLK:(u + 1) * BLK].astype(BF16)
            home_copy(m).start()

    plain = [(0, own, t) for own in (1, 0) for t in range(4)]

    def multiply(sets, order=plain, after=None):
        blank = jnp.zeros((128 - ROWS, BLK), BF16)
        sides, mates = [], []
        for numbers in sets:
            places = [chip_at(m) for m in numbers]
            sides.append(jnp.concatenate(
                [jnp.concatenate([blocks[there], blank], axis=0) for there in places], axis=1
            ))
            mates.append(jnp.concatenate([rights[there] for there in places], axis=1))

        def tile(own, q, span, side, mate):
            holder = core if own == 0 else 1 - core
            rows = jnp.concatenate([lookup[holder, 2 * q], lookup[holder, 2 * q + 1]], axis=0)
            power = jnp.dot(rows, side, preferred_element_type=F32) * LOG2E
            kernel = jnp.exp2(jnp.minimum(power, 0.0)).astype(BF16)
            point_acc[own, :, span] += lax.dot_general(
                mate, kernel, (((1,), (1,)), ((), ())), preferred_element_type=F32
            )
            return jnp.dot(lefts[own, :, span], kernel, preferred_element_type=F32)

        totals = [None for _ in sets]
        for place, (number, own, t) in enumerate(order):
            if after:
                q, span = lax.rem(x + t + 1, 4), part_of(t + 1)
            else:
                q, span = t, slice(t * PART, (t + 1) * PART)
            part = tile(own, q, span, sides[number], mates[number])
            total = totals[number]
            totals[number] = part if total is None else total + part
            if number not in [later[0] for later in order[place + 1:]]:
                send_home(totals[number], sets[number])
            if after:
                after(number, own, t)
        return totals

    def part_of(step):
        return pl.ds(pl.multiple_of(lax.rem(x + step, 4) * PART, PART), PART)

    def swap_part(t):
        return remote(pair_out.at[t], pair_in.at[t], part_send.at[t], part_recv.at[t], pair)

    swap_flag = remote(flag_mine.at[0], flag_pair, pair_send.at[4], pair_recv.at[4], pair)

    def half_of(step, half):
        start = lax.rem(x + step, 4) * PART + half * HALF
        return pl.ds(pl.multiple_of(start, HALF), HALF)

    def x_copy(dx, half):
        return remote(
            x_out.at[dx - 1, half], x_in.at[dx - 1, half],
            x_send.at[dx - 1, half], x_recv.at[dx - 1, half], along_x(dx),
        )

    def chip_sum(dx, half):
        span = half_of(dx, half)
        arrived = pair_in[(dx + 3) % 4, :, half * HALF:(half + 1) * HALF]
        return point_acc[0, :, span] + arrived.astype(F32)

    def send_x(dx):
        for half in range(2):
            x_out[dx - 1, half] = chip_sum(dx, half).astype(BF16)
            x_copy(dx, half).start()

    def leave(number, own, t):
        if own == 1:
            pair_out[t] = point_acc[1, :, part_of(t + 1)].astype(BF16)
            swap_part(t).start()
        if (own, t) == (1, 0):
            swap_flag.start()
        if own == 0 and t < 3:
            swap_part(t).wait_recv()
            send_x(t + 1)

    multiply([[0]])
    block_spread.second()

    def arrive(numbers):
        for m in numbers:
            right_spread.arrive(m)
            block_spread.arrive(m)

    def advance(number):
        later = (number + 3) // 4
        numbers = [
            (1 - later) * (u + 1) + later * (number + 4 * (u + 1)) for u in range(3)
        ]

        @pl.when(number > 0)
        def _():
            arrive(numbers)

        multiply([numbers])

    loop(0, 4, advance)
    numbers = [4, 8, 12]
    arrive(numbers)
    order = [(0, own, t) for own in (1, 0) for t in (1, 0, 2)] + [(0, 1, 3), (0, 0, 3)]
    multiply([numbers], order, leave)

    def flag_x_copy(dx):
        return remote(
            flag_mine.at[1], flag_x.at[dx - 1], fx_send.at[dx - 1], fx_recv.at[dx - 1], along_x(dx)
        )

    swap_flag.wait_recv()
    flag_mine[1] = jnp.maximum(flag_mine[0], flag_pair[...])
    for dx in (1, 2, 3):
        flag_x_copy(dx).start()

    swap_part(3).wait_recv()
    worst = flag_mine[1]
    swap_z = [
        remote(z_out.at[half], z_in.at[half], z_send.at[half], z_recv.at[half], across)
        for half in range(2)
    ]
    for half in range(2):
        total = chip_sum(0, half)
        for dx in (1, 2, 3):
            x_copy(dx, half).wait_recv()
            total = total + x_in[dx - 1, half].astype(F32)
        z_out[half] = total.astype(BF16)
        swap_z[half].start()
    for dx in (1, 2, 3):
        flag_x_copy(dx).wait_recv()
        worst = jnp.maximum(worst, flag_x[dx - 1])
    flag_mine[2] = worst
    flag_across = remote(flag_mine.at[2], flag_z, z_send.at[2], z_recv.at[2], across)
    flag_across.start()

    def back_copy(dx, half):
        return remote(
            back_out.at[half], point_hbm.at[:, half_of(0, half)],
            back_send.at[dx - 1, half], back_recv.at[dx - 1, half], along_x(dx),
        )

    stores = []
    for half in range(2):
        swap_z[half].wait_recv()
        back_out[half] = (z_out[half].astype(F32) + z_in[half].astype(F32)).astype(BF16)
        for dx in (1, 2, 3):
            back_copy(dx, half).start()
        stores.append(pltpu.make_async_copy(
            back_out.at[half], point_hbm.at[:, half_of(0, half)], store_sem.at[half]
        ))
    loop(1, CHIPS, lambda m: home_copy(m).wait_recv())
    centre = own_part[...]
    for m in range(1, CHIPS):
        centre = centre + at_home[m].astype(F32)
    centre_ref[...] = centre

    flag_across.wait_recv()
    flag_ref[...] = jnp.maximum(flag_mine[2], flag_z[...])[0:1, 0:1]
    stores += [
        pltpu.make_async_copy(centre_ref, centre_hbm, store_sem.at[4]),
        pltpu.make_async_copy(flag_ref, flag_hbm, store_sem.at[5]),
    ]
    for store in stores:
        store.start()

    def drain(m):
        idx_copy(m).wait_send()
        right_spread.drain(m)
        block_spread.drain(m)
        home_copy(m).wait_send()

    loop(1, CHIPS, drain)
    each_round(lambda turn, m: row_copy(turn, m).wait_send())
    for copy in (swap_lookup, swap_left, swap_flag, *swap_z, flag_across):
        copy.wait_send()
    for t in range(4):
        swap_part(t).wait_send()
    for dx in (1, 2, 3):
        for half in range(2):
            x_copy(dx, half).wait_send()
        flag_x_copy(dx).wait_send()

    for half in range(2):
        for dx in (1, 2, 3):
            remote(
                back_out.at[half], point_hbm.at[:, half_of(4 - dx, half)],
                back_send.at[dx - 1, half], back_recv.at[dx - 1, half], along_x(dx),
            ).wait_recv()
            back_copy(dx, half).wait_send()
    for store in stores:
        store.wait()


def fused(rounds, points, centre_index, inv_scale, left_cols, right_cols):
    anywhere = pl.BlockSpec(memory_space=pl.ANY)
    dma = pltpu.SemaphoreType.DMA
    buf = pltpu.VMEM
    return pl.pallas_call(
        functools.partial(fused_kernel, rounds),
        out_shape=(
            jax.ShapeDtypeStruct((COLS, HERE), BF16),
            jax.ShapeDtypeStruct((COLS, BLK), F32),
            jax.ShapeDtypeStruct((1, 1), F32),
        ),
        in_specs=[anywhere] * 5,
        out_specs=[anywhere] * 3,
        scratch_shapes=[
            buf((FEAT, HERE), F32),
            buf((1, FEAT), F32),
            buf((COLS, BLK), F32),
            buf((1, 1), F32),
            dma((5,)),
            dma((6,)),
            buf((CHIPS, 1, BLK), I32),
            buf((CHIPS, 1, BLK), F32),
            buf((128, HERE), F32),
            buf((2, 8, 256, 128), BF16),
            buf((rounds, CHIPS, SLOTS, 128), BF16),
            buf((rounds, CHIPS, SLOTS, 128), BF16),
            buf((2, COLS, HERE), BF16),
            buf((CHIPS, ROWS, BLK), BF16),
            buf((CHIPS, COLS, BLK), BF16),
            buf((2, COLS, HERE), F32),
            buf((COLS, BLK), F32),
            buf((CHIPS, COLS, BLK), BF16),
            buf((CHIPS, COLS, BLK), BF16),
            buf((4, COLS, PART), BF16),
            buf((4, COLS, PART), BF16),
            buf((3, 2, COLS, HALF), BF16),
            buf((3, 2, COLS, HALF), BF16),
            buf((2, COLS, HALF), BF16),
            buf((2, COLS, HALF), BF16),
            buf((2, COLS, HALF), BF16),
            buf((3, 8, 128), F32),
            buf((8, 128), F32),
            buf((3, 8, 128), F32),
            buf((8, 128), F32),
        ]
        + [dma((CHIPS,))] * 2
        + [dma((rounds, CHIPS))] * 2
        + [dma((CHIPS,))] * 6
        + [dma((5,)), dma((5,)), dma((4,)), dma((4,)), dma((3, 2)), dma((3, 2)), dma((3,)), dma((3,))]
        + [dma((3, 2))] * 2
        + [dma((3,))] * 2,
        compiler_params=pltpu.CompilerParams(
            collective_id=rounds, has_side_effects=True, vmem_limit_bytes=VMEM_LIMIT
        ),
        name=f"nystrom_products_{rounds}",
    )(points, inv_scale[None, :], centre_index[None, :], left_cols, right_cols)


ROUNDS = -(-BLK // SLOTS)


def body(*arguments):
    point_side, centre_side, most = fused(1, *arguments)
    point_side, centre_side = lax.cond(
        most[0, 0] > SLOTS, lambda: fused(ROUNDS, *arguments)[:2], lambda: (point_side, centre_side)
    )
    return point_side.astype(F32), centre_side


def solution(mesh):
    return jax.shard_map(
        body,
        mesh=mesh,
        in_specs=(P(None, "pts"), P(("ctr", "pts")), P(), P(None, "pts"), P(None, ("ctr", "pts"))),
        out_specs=(P(None, "pts"), P(None, ("ctr", "pts"))),
        check_vma=False,
    )
```
